1024 devices in a mesh: pool: 2 (over core), group: 8 (over z), ep: 64 (over y, x).
Axes of the slice: x: 8, y: 8, z: 8, core: 2. Of those that a mesh axis runs over, the one named last changes fastest.
Arguments:
- moe_in: bfloat16 [8192, 2048], P(('group', 'ep')), may hold values from -6 to 6
- out_grad: bfloat16 [8192, 2048], P(('group', 'ep')), may hold values from -6 to 6
- gates: float32 [8192, 8], P(('group', 'ep')), may hold values from 0.1 to 1
- routes: int32 [8192, 8], P(('group', 'ep')), may hold values from 0 to 63, all different within a row; in each aligned block of 16 rows (0 to 15, 16 to 31, ...) at most 4 rows name the same one
- w_gate: bfloat16 [64, 2048, 768], P('ep', None, 'pool'), may hold values from -0.125 to 0.125
- w_up: bfloat16 [64, 2048, 768], P('ep', None, 'pool'), may hold values from -0.125 to 0.125
- w_down: bfloat16 [64, 768, 2048], P('ep', 'pool'), may hold values from -0.21875 to 0.21875
- context_t: bfloat16 [4096, 8192], P('ep', 'group'), may hold values from -0.0625 to 0.0625
Outputs:
- hidden_grad: float32 [8192, 2048], P(('group', 'ep'), 'pool')
- wo_grad: float32 [4096, 2048], P('ep', ('pool', 'group'))
The draws below stay inside these ranges and needn't reach their ends.
Inputs may be any that keep to these rules, and one draw needn't show every extreme that they name: `routes`: each row names 8 different experts. Among the 16 rows of one index of group and ep no expert is named more than 4 times, a bound that some block reaches.
All inputs are finite; a program needn't handle non-finite values.
Results may differ from the reference program's by a relative error of at most 0.0045.
Values may be sent and summed in bfloat16 or wider, within the bound.
No kernel may reach another device: no remote copies, remote signals or barrier semaphores. Data moves between devices by JAX's collectives and lax.ppermute only.
A program may use at most 32 MiB of HBM per device.

```python
import math
import jax
import jax.numpy as jnp
import numpy as np
from jax import lax

D = 2048
F = 768
TOK_DEV = 16
HQ = 4096
EXPERTS = 64
TOP = 8
CAP = 4
TOKENS = 8192
N_GROUP = 8
N_EP = 64


def shard_levels(own_key, shape, split, smallest, high):
    loudness, own = 1.0, jax.random.fold_in(own_key, 6)
    for axis_at, shards_of in split:
        steps = jnp.exp(jax.random.uniform(jax.random.fold_in(own, axis_at), (shards_of,), jnp.float32, smallest / len(split), high / len(split)))
        loudness = loudness * jnp.repeat(steps, shape[axis_at] // shards_of).reshape([-1 if axis == axis_at else 1 for axis in range(len(shape))])
    return loudness


def routed_block(key, own, number, rows, number_of, top, reach, slope):
    sequence = jax.random.permutation(key, number_of)
    crowded, ordinary = portions_of(number_of, rows * top, reach, slope, True), portions_of(number_of, rows * top, reach, slope, False)
    places = jnp.arange(number_of)

    def named(lengths, rotation):
        used = int((lengths > 0).sum())
        fixed = max(1, used // 4)
        shifted = fixed + (places - fixed + rotation * (used - fixed)) % max(1, number_of - fixed)
        return jnp.zeros((number_of,), jnp.int32).at[sequence[jnp.where(places < fixed, places, shifted)]].set(jnp.asarray(lengths, jnp.int32))

    lengths = jnp.where(number % 4 == 0, named(crowded, number // 4), named(ordinary, number - number // 4 - 1))
    mixed = jax.random.permutation(jax.random.fold_in(own, 3), number_of)
    source_of, sink = mixed[0:number_of // 2 * 2:2], mixed[1:number_of // 2 * 2:2]
    slack = jnp.minimum(lengths[source_of] - 1, reach - lengths[sink]) // 2
    slack = jnp.where((source_of == sequence[0]) | (sink == sequence[0]) | (lengths[sink] == 0), 0, jnp.maximum(slack, 0))
    shifted = jax.random.randint(jax.random.fold_in(own, 4), (number_of // 2,), 0, 1 << 20) % (slack + 1)
    lengths = lengths.at[source_of].add(-shifted).at[sink].add(shifted)
    labels = jnp.searchsorted(jnp.cumsum(lengths), jnp.arange(rows * top), side="right").astype(jnp.int32)
    listing = labels.reshape(top, rows).T
    listing = listing[jax.random.permutation(jax.random.fold_in(own, 1), rows)]
    rotation = jax.random.randint(jax.random.fold_in(own, 2), (rows, 1), 0, top)
    return jnp.take_along_axis(listing, (jnp.arange(top)[None, :] + rotation) % top, axis=1)


def portions_of(count, total, reach, slope, full):
    portions = [(1 << 20) // math.isqrt(standing ** slope) + 1 for standing in range(1, count + 1)]
    largest = reach if full else min(reach, max(-(-total // count), total * portions[0] // sum(portions)))
    least = 1 if total - largest >= count - 1 else 0
    given, surplus = [largest] + [least] * (count - 1), total - largest - least * (count - 1)
    while surplus > 0:
        candidates = [i for i in range(1, count) if given[i] < largest] or [i for i in range(1, count) if given[i] < reach]
        whole, remaining = sum([portions[i] for i in candidates]), surplus
        for i in candidates:
            extra = min(reach - given[i], max(1, remaining * portions[i] // whole), surplus)
            given[i] = given[i] + extra
            surplus = surplus - extra
    return np.array(given)


def normal_values(stream_key, shape, spread, reach, split=(), kind=jnp.bfloat16):
    gain = shard_levels(stream_key, shape, split, -0.22, 0.18) if split else 1.0
    array = jax.random.normal(stream_key, shape, jnp.float32) * spread * gain
    return jnp.minimum(jnp.maximum(array, -reach), reach).astype(kind)


def setup_inputs(seed: int = 0) -> dict:
    streams_of = jax.random.split(jax.random.key(seed), 9)
    moe_in = normal_values(streams_of[0], (TOKENS, D), 1.0, 6.0, ((0, 512),))
    out_grad = normal_values(streams_of[1], (TOKENS, D), 1.0, 6.0, ((0, 512),))
    gates = jnp.clip(jnp.exp(math.log(1.0) - 2.3025851 * jax.random.uniform(streams_of[2], (TOKENS, TOP), jnp.float32) ** shard_levels(streams_of[2], (TOKENS, TOP), ((0, 512),), -0.2, 0.2)), 0.1, 1.0)
    routes_keys = jax.random.split(jax.random.fold_in(streams_of[3], 1), TOKENS // TOK_DEV)
    routes_turns = jax.random.permutation(jax.random.fold_in(streams_of[3], 3), TOKENS // TOK_DEV)
    routes = jax.vmap(lambda own, number: routed_block(jax.random.fold_in(streams_of[3], 2), own, number, TOK_DEV, EXPERTS, TOP, CAP, 2))(routes_keys, routes_turns).reshape((TOKENS, TOP))
    w_gate = normal_values(streams_of[4], (EXPERTS, D, F), D ** -0.5, 0.125, ((0, 64), (2, 2)))
    w_up = normal_values(streams_of[5], (EXPERTS, D, F), D ** -0.5, 0.125, ((0, 64), (2, 2)))
    w_down = normal_values(streams_of[6], (EXPERTS, F, D), F ** -0.5, 0.21875, ((0, 64), (1, 2)))
    context_t = normal_values(streams_of[7], (HQ, TOKENS), TOKENS ** -0.5, 0.0625, ((0, 64), (1, 8)))
    return {"moe_in": moe_in, "out_grad": out_grad, "gates": gates, "routes": routes, "w_gate": w_gate, "w_up": w_up, "w_down": w_down, "context_t": context_t}


def dot_transposed(left, right):
    return lax.dot_general(left, right, (((1,), (1,)), ((), ())), preferred_element_type=jnp.float32)

def half_input_grad(inputs_rows, grads_rows, gate_matrix, up_matrix, down_matrix):
    gate_value = jnp.dot(inputs_rows, gate_matrix, preferred_element_type=jnp.float32)
    up_value = jnp.dot(inputs_rows, up_matrix, preferred_element_type=jnp.float32)
    act_grad = dot_transposed(grads_rows, down_matrix)
    sigmoid_gate = jax.nn.sigmoid(gate_value)
    up_grad = (act_grad * gate_value * sigmoid_gate).astype(jnp.bfloat16)
    gate_grad = (act_grad * up_value * sigmoid_gate * (1.0 + gate_value * (1.0 - sigmoid_gate))).astype(jnp.bfloat16)
    input_grad = dot_transposed(gate_grad, gate_matrix) + dot_transposed(up_grad, up_matrix)
    return input_grad.astype(jnp.bfloat16)

def reference(moe_in, out_grad, gates, routes, w_gate, w_up, w_down, context_t):
    pair_count = TOKENS * TOP
    half_hidden = F // 2
    expert_ids = routes.reshape(pair_count)
    token_of_pair = (jnp.arange(pair_count, dtype=jnp.int32) // TOP).astype(jnp.int32)
    sorted_pairs = jnp.argsort(expert_ids, stable=True).astype(jnp.int32)
    counts = lax.optimization_barrier(jnp.sum((expert_ids[:, None] == jnp.arange(EXPERTS, dtype=jnp.int32)[None, :]).astype(jnp.int32), axis=0)).astype(jnp.int32)
    starts = (jnp.cumsum(counts) - counts).astype(jnp.int32)
    most_rows = CAP * N_EP * N_GROUP
    padded_pairs = jnp.concatenate([sorted_pairs, jnp.zeros((most_rows,), jnp.int32)])
    gate_flat = gates.reshape(pair_count)

    def per_expert(summed, expert):
        pair_index = lax.dynamic_slice_in_dim(padded_pairs, starts[expert], most_rows)
        live_rows = jnp.arange(most_rows, dtype=jnp.int32) < counts[expert]
        token_rows = jnp.take(token_of_pair, pair_index)
        inputs_rows = jnp.take(moe_in, token_rows, axis=0)
        grads_rows = jnp.take(out_grad, token_rows, axis=0)
        gate_all = w_gate[expert]
        up_all = w_up[expert]
        down_all = w_down[expert]
        total = jnp.zeros((most_rows, D), jnp.float32)
        for half in range(2):
            low = half * half_hidden
            piece = half_input_grad(inputs_rows, grads_rows, gate_all[:, low:low + half_hidden], up_all[:, low:low + half_hidden], down_all[low:low + half_hidden, :])
            total = total + piece.astype(jnp.float32)
        weight_rows = jnp.where(live_rows, jnp.take(gate_flat, pair_index), jnp.float32(0.0))
        summed = summed.at[token_rows].add(weight_rows[:, None] * total)
        return (summed, None)
    moe_grad, _ = lax.scan(per_expert, jnp.zeros((TOKENS, D), jnp.float32), jnp.arange(EXPERTS, dtype=jnp.int32))
    hidden_grad = out_grad.astype(jnp.float32) + moe_grad
    wo_grad = jnp.dot(context_t, hidden_grad.astype(jnp.bfloat16), preferred_element_type=jnp.float32)
    return (hidden_grad, wo_grad)
```

```python
import jax
import jax.numpy as jnp
from jax import lax
from jax.sharding import Mesh, PartitionSpec as P

ROWS = 8
BF = jnp.bfloat16
F32 = jnp.float32


def dot_f32(left, right):
    return jnp.dot(left, right, preferred_element_type=F32)


def dot_transposed(left, right):
    return lax.dot_general(left, right, (((1,), (1,)), ((), ())), preferred_element_type=F32)


def half_input_grad(inputs_rows, grads_rows, gate_matrix, up_matrix, down_matrix):
    gate_value = dot_f32(inputs_rows, gate_matrix)
    up_value = dot_f32(inputs_rows, up_matrix)
    act_grad = dot_transposed(grads_rows, down_matrix)
    sigmoid_gate = jax.nn.sigmoid(gate_value)
    up_grad = (act_grad * gate_value * sigmoid_gate).astype(BF)
    gate_grad = (
        act_grad * up_value * sigmoid_gate * (1.0 + gate_value * (1.0 - sigmoid_gate))
    ).astype(BF)
    return dot_transposed(gate_grad, gate_matrix) + dot_transposed(up_grad, up_matrix)


def swap_pool(value):
    return lax.ppermute(value, "pool", ((0, 1), (1, 0)))


def exchange(value, axes):
    return lax.all_to_all(value, axes, split_axis=0, concat_axis=0, tiled=True)


def per_device(moe_in, out_grad, gates, routes, w_gate, w_up, w_down, context_t):
    tok_rows, model_width = moe_in.shape
    top_count = routes.shape[1]
    y_size, x_size, z_size = lax.axis_size("y"), lax.axis_size("x"), lax.axis_size("group")
    experts = y_size * x_size
    capacity = 2 * tok_rows * top_count // experts
    own_slots = capacity // 2
    pool_index = lax.axis_index("pool")
    half_width = model_width // 2
    pair_count = tok_rows * top_count

    expert_ids = routes.reshape(pair_count)
    hits = (expert_ids[:, None] == jnp.arange(experts, dtype=jnp.int32)[None, :]).astype(jnp.int32)
    earlier = jnp.cumsum(hits, axis=0) - hits
    position = jnp.sum(earlier * hits, axis=1)
    own = position // own_slots == pool_index
    slot_ids = jnp.where(own, expert_ids * own_slots + position % own_slots, -1)
    slot_ids = slot_ids.reshape(tok_rows, top_count)
    slot_grid = jnp.arange(experts * own_slots, dtype=jnp.int32)
    placed = slot_ids[:, :, None] == slot_grid[None, None, :]
    picker = jnp.any(placed, axis=1).astype(BF)
    weights = jnp.sum(jnp.where(placed, gates[:, :, None], 0.0), axis=1)

    piece_width = 2 * model_width * own_slots // ROWS
    parts = 2 * model_width // piece_width
    stacked = jnp.concatenate(
        [a[:, i * piece_width:(i + 1) * piece_width] for a in (moe_in, out_grad) for i in range(parts // 2)], 0
    )
    eye = jnp.eye(parts, dtype=BF)
    spread = (picker.T[:, None, None, :] * eye[None, :, :, None]).reshape(
        experts * ROWS, parts * tok_rows
    )
    send = dot_f32(spread, stacked).astype(BF).reshape(experts, ROWS, piece_width)
    send, context_t, weights = lax.optimization_barrier((send, context_t, weights))
    received = exchange(send, ("y", "x"))
    other_gate, other_up, other_down = swap_pool(w_gate[0]), swap_pool(w_up[0]), swap_pool(w_down[0])
    heads, tokens = context_t.shape
    wide = tokens // y_size
    context_y = exchange(
        jnp.stack([context_t[:, i * wide:(i + 1) * wide] for i in range(y_size)]), "y"
    )
    received, context_y = lax.optimization_barrier((received, context_y))
    context_all = lax.all_gather(context_y.reshape(y_size * heads, wide), "group", axis=0, tiled=False)

    rows = received.reshape(experts * own_slots, 2, model_width)
    inputs_rows, grads_rows = rows[:, 0], rows[:, 1]
    total = half_input_grad(inputs_rows, grads_rows, w_gate[0], w_up[0], w_down[0]).astype(BF).astype(
        F32
    ) + half_input_grad(inputs_rows, grads_rows, other_gate, other_up, other_down).astype(BF).astype(F32)
    back_width = model_width * own_slots // ROWS
    back_parts = model_width // back_width
    back = total.astype(BF).reshape(experts, ROWS, back_width)
    returned = exchange(back, ("y", "x"))

    high = lax.reduce_precision(weights, 8, 7).astype(BF)
    low = (weights - high.astype(F32)).astype(BF)
    both = jnp.stack((high, low))
    back_eye = jnp.eye(back_parts, dtype=BF)
    mixer = (both[None, :, :, :, None] * back_eye[:, None, None, None, :]).reshape(
        back_parts * 2 * tok_rows, experts * ROWS
    )
    mixed = dot_f32(mixer, returned.reshape(experts * ROWS, back_width))
    mixed = jnp.sum(mixed.reshape(back_parts, 2, tok_rows, back_width), axis=1)
    per_half = back_parts // 2
    mine = lax.dynamic_slice_in_dim(mixed, pool_index * per_half, per_half, 0)
    theirs = lax.dynamic_slice_in_dim(mixed, (1 - pool_index) * per_half, per_half, 0)
    moe_part = mine + swap_pool(theirs)
    moe_part = jnp.concatenate([moe_part[i] for i in range(per_half)], axis=1)
    grad_half = lax.dynamic_slice_in_dim(out_grad, pool_index * half_width, half_width, 1)
    hidden_grad = grad_half.astype(F32) + moe_part
    hidden_grad_b = hidden_grad.astype(BF)

    cols = half_width // z_size
    by_column = jnp.stack([hidden_grad_b[:, i * cols:(i + 1) * cols] for i in range(z_size)])
    by_group = exchange(by_column, "group")
    gathered_b = exchange(
        jnp.broadcast_to(by_group[None], (x_size, z_size, tok_rows, cols)).reshape(
            x_size, z_size * tok_rows, cols
        ),
        "x",
    )
    tokens_b = gathered_b.reshape(x_size, z_size, tok_rows, cols).transpose(1, 0, 2, 3)
    rows_c = jnp.concatenate([context_all[i] for i in range(z_size)], axis=1)
    partial_wo = dot_f32(rows_c, tokens_b.reshape(-1, cols)).astype(BF)
    terms = exchange(partial_wo.reshape(y_size, heads, cols), "y")
    wo_grad = jnp.sum(terms.astype(F32), axis=0)
    return (hidden_grad, wo_grad)


def solution(mesh):
    pool, group, ep = (mesh.shape[name] for name in ("pool", "group", "ep"))
    y_size = 8
    grid = Mesh(mesh.devices.reshape(pool, group, y_size, ep // y_size), ("pool", "group", "y", "x"))
    tokens = ("group", "y", "x")
    return jax.shard_map(
        per_device,
        mesh=grid,
        in_specs=(
            P(tokens, None),
            P(tokens, None),
            P(tokens, None),
            P(tokens, None),
            P(("y", "x"), None, "pool"),
            P(("y", "x"), None, "pool"),
            P(("y", "x"), "pool", None),
            P(("y", "x"), "group"),
        ),
        out_specs=(P(tokens, "pool"), P(("y", "x"), ("pool", "group"))),
        check_vma=False,
    )
```

```python
import jax
import jax.numpy as jnp
from jax import lax
from jax.experimental import pallas as pl
from jax.experimental.pallas import tpu as pltpu
from jax.sharding import Mesh, PartitionSpec as P

ROWS = 8
BF = jnp.bfloat16
F32 = jnp.float32


def dot_f32(left, right):
    return jnp.dot(left, right, preferred_element_type=F32)


def dot_transposed(left, right):
    return lax.dot_general(left, right, (((1,), (1,)), ((), ())), preferred_element_type=F32)


def moved(rows_out, rows_in, source):
    at = lax.broadcasted_iota(jnp.int32, (rows_out, rows_in), 0)
    of = lax.broadcasted_iota(jnp.int32, (rows_out, rows_in), 1)
    return (of == source(at)).astype(BF)


def expert_kernel(rows_ref, *refs):
    weights, out_ref, held, sems = refs[:6], refs[6], refs[7:13], refs[13]
    copies = [pltpu.make_async_copy(w, h, sems.at[i]) for i, (w, h) in enumerate(zip(weights, held))]
    for copy in copies:
        copy.start()
    total_rows, piece = rows_ref.shape
    width = held[0].shape[0]
    parts = 2 * width // piece
    slots = total_rows // parts
    to_parts = moved(total_rows, total_rows, lambda i: lax.rem(i, slots) * parts + lax.div(i, slots))
    sorted_rows = dot_f32(to_parts, rows_ref[...]).astype(BF)
    part = [sorted_rows[i * slots:(i + 1) * slots] for i in range(parts)]
    inputs_rows = jnp.concatenate(part[:parts // 2], axis=1)
    grads_rows = jnp.concatenate(part[parts // 2:], axis=1)
    total = None
    for half in range(2):
        gate_ref, up_ref, down_ref = held[3 * half:3 * half + 3]
        copies[3 * half].wait()
        gate_value = dot_f32(inputs_rows, gate_ref[...])
        copies[3 * half + 1].wait()
        up_value = dot_f32(inputs_rows, up_ref[...])
        copies[3 * half + 2].wait()
        act_grad = dot_transposed(grads_rows, down_ref[...])
        sigmoid_gate = jax.nn.sigmoid(gate_value)
        up_grad = (act_grad * gate_value * sigmoid_gate).astype(BF)
        gate_grad = (
            act_grad * up_value * sigmoid_gate * (1.0 + gate_value * (1.0 - sigmoid_gate))
        ).astype(BF)
        half_grad = dot_transposed(gate_grad, gate_ref[...]) + dot_transposed(up_grad, up_ref[...])
        total = half_grad if total is None else total + half_grad
    total = total.astype(BF)
    back = out_ref.shape[1]
    pieces = width // back
    stacked = jnp.concatenate([total[:, i * back:(i + 1) * back] for i in range(pieces)], axis=0)
    to_slots = moved(
        slots * pieces, slots * pieces, lambda i: lax.rem(i, pieces) * slots + lax.div(i, pieces)
    )
    out_ref[...] = dot_f32(to_slots, stacked).astype(BF)


def expert_rows(rows, weights, back):
    width = weights[0].shape[0]
    slots = rows.size // (2 * width)
    hidden = weights[0].shape[1]
    vmem = pl.BlockSpec(memory_space=pltpu.VMEM)
    anywhere = pl.BlockSpec(memory_space=pltpu.HBM)
    return pl.pallas_call(
        expert_kernel,
        out_shape=jax.ShapeDtypeStruct((slots * width // back, back), BF),
        in_specs=[vmem] + [anywhere] * 6,
        out_specs=vmem,
        scratch_shapes=[pltpu.VMEM(w.shape, BF) for w in weights] + [pltpu.SemaphoreType.DMA((6,))],
        compiler_params=pltpu.CompilerParams(vmem_limit_bytes=50 * 2**20),
        cost_estimate=pl.CostEstimate(
            flops=2 * slots * width * hidden * 10,
            bytes_accessed=12 * width * hidden,
            transcendentals=2 * slots * hidden,
        ),
        name="expert",
    )(rows, *weights)


def product_kernel(*refs):
    contexts, tokens_ref, out_ref = refs[:-2], refs[-2], refs[-1]
    x_size, depth, cols = tokens_ref.shape
    tok = depth // sum(ref.shape[0] for ref in contexts)
    total, at = None, 0
    for ref in contexts:
        for i in range(ref.shape[0]):
            tokens = tokens_ref[:, at * tok:(at + 1) * tok, :].reshape(x_size * tok, cols)
            term = dot_f32(ref[i], tokens)
            total = term if total is None else total + term
            at += 1
    out_ref[...] = total.astype(BF)


def context_product(contexts, tokens_b):
    rows, depth = contexts[0].shape[1:]
    groups = sum(c.shape[0] for c in contexts)
    cols = tokens_b.shape[2]
    return pl.pallas_call(
        product_kernel,
        out_shape=jax.ShapeDtypeStruct((rows, cols), BF),
        in_specs=[pl.BlockSpec(memory_space=pltpu.VMEM)] * (len(contexts) + 1),
        out_specs=pl.BlockSpec(memory_space=pltpu.VMEM),
        compiler_params=pltpu.CompilerParams(vmem_limit_bytes=16 * 2**20),
        cost_estimate=pl.CostEstimate(
            flops=2 * groups * rows * depth * cols, bytes_accessed=2 * groups * rows * depth, transcendentals=0
        ),
        name="context_product",
    )(*contexts, tokens_b)


def swap_pool(value):
    return lax.ppermute(value, "pool", ((0, 1), (1, 0)))


def exchange(value, axes):
    return lax.all_to_all(value, axes, split_axis=0, concat_axis=0, tiled=True)


def spread_over_y(context_t, y_index, y_size):
    wide = context_t.shape[1] // y_size
    places = [
        lax.dynamic_slice_in_dim(context_t, jnp.bitwise_xor(y_index, r) * wide, wide, 1)
        for r in range(y_size)
    ]
    bit = 1
    while bit < y_size:
        crossing = [r for r in range(y_size) if r & bit]
        came = lax.ppermute(
            jnp.stack([places[r] for r in crossing]), "y", tuple((s, s ^ bit) for s in range(y_size))
        )
        for i, r in enumerate(crossing):
            places[r] = came[i]
        bit *= 2
    order = jnp.bitwise_xor(y_index, jnp.arange(y_size, dtype=jnp.int32))
    return jnp.take(jnp.stack(places), order, axis=0)


def across_group(block, z_size, bit):
    return lax.ppermute(block, "group", tuple((s, s ^ bit) for s in range(z_size)))


def spread_over_group(pieces, z_index, z_size):
    bit = z_size // 2
    order = [0, bit]
    while bit > 1:
        bit //= 2
        pieces = pieces + [across_group(jnp.concatenate(pieces, axis=0), z_size, bit)]
        order += [r ^ bit for r in order]
    return pieces, jnp.bitwise_xor(z_index, jnp.asarray(order, jnp.int32))


def per_device(moe_in, out_grad, gates, routes, w_gate, w_up, w_down, context_t):
    tok_rows, model_width = moe_in.shape
    top_count = routes.shape[1]
    y_size, x_size, z_size = lax.axis_size("y"), lax.axis_size("x"), lax.axis_size("group")
    experts = y_size * x_size
    capacity = 2 * tok_rows * top_count // experts
    own_slots = capacity // 2
    pool_index = lax.axis_index("pool")
    y_index = lax.axis_index("y")
    half_width = model_width // 2
    pair_count = tok_rows * top_count

    expert_ids = routes.reshape(pair_count)
    hits = (expert_ids[:, None] == jnp.arange(experts, dtype=jnp.int32)[None, :]).astype(jnp.int32)
    earlier = jnp.cumsum(hits, axis=0) - hits
    position = jnp.sum(earlier * hits, axis=1)
    own = position // own_slots == pool_index
    slot_ids = jnp.where(own, expert_ids * own_slots + position % own_slots, -1)
    slot_ids = slot_ids.reshape(tok_rows, top_count)
    slot_grid = jnp.arange(experts * own_slots, dtype=jnp.int32)
    placed = slot_ids[:, :, None] == slot_grid[None, None, :]
    picker = jnp.any(placed, axis=1).astype(BF)
    weights = jnp.sum(jnp.where(placed, gates[:, :, None], 0.0), axis=1)

    piece_width = 2 * model_width * own_slots // ROWS
    parts = 2 * model_width // piece_width
    stacked = jnp.concatenate(
        [a[:, i * piece_width:(i + 1) * piece_width] for a in (moe_in, out_grad) for i in range(parts // 2)], 0
    )
    eye = jnp.eye(parts, dtype=BF)
    spread = (picker.T[:, None, None, :] * eye[None, :, :, None]).reshape(
        experts * ROWS, parts * tok_rows
    )
    send = dot_f32(spread, stacked).astype(BF).reshape(experts, ROWS, piece_width)
    send, context_t, weights = lax.optimization_barrier((send, context_t, weights))
    received = exchange(send, ("y", "x"))
    other_gate, other_up, other_down = swap_pool(w_gate[0]), swap_pool(w_up[0]), swap_pool(w_down[0])
    heads = context_t.shape[0]
    context_y = spread_over_y(context_t, y_index, y_size).reshape(1, y_size * heads, -1)
    z_index = lax.axis_index("group")
    context_pair = [context_y, across_group(context_y, z_size, z_size // 2)]
    received, context_pair = lax.optimization_barrier((received, context_pair))
    context_all, group_order = spread_over_group(context_pair, z_index, z_size)

    back_width = model_width * own_slots // ROWS
    back_parts = model_width // back_width
    back = expert_rows(
        received.reshape(experts * ROWS, piece_width),
        (w_gate[0], w_up[0], w_down[0], other_gate, other_up, other_down),
        back_width,
    ).reshape(experts, ROWS, back_width)
    returned = exchange(back, ("y", "x"))
    returned, context_all = lax.optimization_barrier((returned, context_all))

    high = lax.reduce_precision(weights, 8, 7).astype(BF)
    low = (weights - high.astype(F32)).astype(BF)
    both = jnp.stack((high, low))
    back_eye = jnp.eye(back_parts, dtype=BF)
    mixer = (both[None, :, :, :, None] * back_eye[:, None, None, None, :]).reshape(
        back_parts * 2 * tok_rows, experts * ROWS
    )
    mixed = dot_f32(mixer, returned.reshape(experts * ROWS, back_width))
    mixed = jnp.sum(mixed.reshape(back_parts, 2, tok_rows, back_width), axis=1)
    per_half = back_parts // 2
    mine = lax.dynamic_slice_in_dim(mixed, pool_index * per_half, per_half, 0)
    theirs = lax.dynamic_slice_in_dim(mixed, (1 - pool_index) * per_half, per_half, 0)
    moe_part = mine + swap_pool(theirs)
    moe_part = jnp.concatenate([moe_part[i] for i in range(per_half)], axis=1)
    grad_half = lax.dynamic_slice_in_dim(out_grad, pool_index * half_width, half_width, 1)
    hidden_grad = grad_half.astype(F32) + moe_part
    hidden_grad_b = hidden_grad.astype(BF)

    cols = half_width // z_size
    by_column = jnp.stack([hidden_grad_b[:, i * cols:(i + 1) * cols] for i in range(z_size)])
    by_group = jnp.take(exchange(by_column, "group"), group_order, axis=0)
    gathered_b = exchange(
        jnp.broadcast_to(by_group[None], (x_size, z_size, tok_rows, cols)).reshape(
            x_size, z_size * tok_rows, cols
        ),
        "x",
    )
    partial_wo = context_product(context_all, gathered_b)
    terms = exchange(partial_wo.reshape(y_size, heads, cols), "y")
    wo_grad = jnp.sum(terms.astype(F32), axis=0)
    return (hidden_grad, wo_grad)


def solution(mesh):
    pool, group, ep = (mesh.shape[name] for name in ("pool", "group", "ep"))
    y_size = 8
    grid = Mesh(mesh.devices.reshape(pool, group, y_size, ep // y_size), ("pool", "group", "y", "x"))
    tokens = ("group", "y", "x")
    return jax.shard_map(
        per_device,
        mesh=grid,
        in_specs=(
            P(tokens, None),
            P(tokens, None),
            P(tokens, None),
            P(tokens, None),
            P(("y", "x"), None, "pool"),
            P(("y", "x"), None, "pool"),
            P(("y", "x"), "pool", None),
            P(("y", "x"), "group"),
        ),
        out_specs=(P(tokens, "pool"), P(("y", "x"), ("pool", "group"))),
        check_vma=False,
    )
```

```python
import jax
import jax.numpy as jnp
from jax import lax
from jax.experimental import pallas as pl
from jax.experimental.pallas import tpu as pltpu
from jax.sharding import Mesh, PartitionSpec as P

ROWS = 8
SORT = 256
BF = jnp.bfloat16
F32 = jnp.float32


def dot_f32(left, right):
    return jnp.dot(left, right, preferred_element_type=F32)


def dot_transposed(left, right):
    return lax.dot_general(left, right, (((1,), (1,)), ((), ())), preferred_element_type=F32)


def moved(rows_out, rows_in, source):
    at = lax.broadcasted_iota(jnp.int32, (rows_out, rows_in), 0)
    of = lax.broadcasted_iota(jnp.int32, (rows_out, rows_in), 1)
    return (of == source(at)).astype(BF)


def expert_kernel(rows_ref, *refs):
    weights, out_ref, held, sems = refs[:6], refs[6], refs[7:13], refs[13]
    copies = [pltpu.make_async_copy(w, h, sems.at[i]) for i, (w, h) in enumerate(zip(weights, held))]
    for copy in copies:
        copy.start()
    total_rows, piece = rows_ref.shape
    width = held[0].shape[0]
    parts = 2 * width // piece
    block = min(SORT, total_rows)
    slots = block // parts
    to_parts = moved(block, block, lambda i: lax.rem(i, slots) * parts + lax.div(i, slots))
    sorted_rows = [
        dot_f32(to_parts, rows_ref[i:i + block]).astype(BF) for i in range(0, total_rows, block)
    ]
    part = [
        jnp.concatenate([rows[i * slots:(i + 1) * slots] for rows in sorted_rows], axis=0)
        for i in range(parts)
    ]
    inputs_rows = jnp.concatenate(part[:parts // 2], axis=1)
    grads_rows = jnp.concatenate(part[parts // 2:], axis=1)
    total = None
    for half in range(2):
        gate_ref, up_ref, down_ref = held[3 * half:3 * half + 3]
        copies[3 * half].wait()
        gate_value = dot_f32(inputs_rows, gate_ref[...])
        copies[3 * half + 1].wait()
        up_value = dot_f32(inputs_rows, up_ref[...])
        copies[3 * half + 2].wait()
        act_grad = dot_transposed(grads_rows, down_ref[...])
        sigmoid_gate = jax.nn.sigmoid(gate_value)
        up_grad = (act_grad * gate_value * sigmoid_gate).astype(BF)
        gate_grad = (
            act_grad * up_value * sigmoid_gate * (1.0 + gate_value * (1.0 - sigmoid_gate))
        ).astype(BF)
        half_grad = dot_transposed(gate_grad, gate_ref[...]) + dot_transposed(up_grad, up_ref[...])
        total = half_grad if total is None else total + half_grad
    total = total.astype(BF)
    back = out_ref.shape[1]
    pieces = width // back
    block = min(SORT, out_ref.shape[0])
    slots = block // pieces
    to_slots = moved(block, block, lambda i: lax.rem(i, pieces) * slots + lax.div(i, pieces))
    for at in range(out_ref.shape[0] // block):
        rows = total[at * slots:(at + 1) * slots]
        stacked = jnp.concatenate([rows[:, i * back:(i + 1) * back] for i in range(pieces)], axis=0)
        out_ref[at * block:(at + 1) * block] = dot_f32(to_slots, stacked).astype(BF)


def expert_rows(rows, weights, back):
    width = weights[0].shape[0]
    slots = rows.size // (2 * width)
    hidden = weights[0].shape[1]
    vmem = pl.BlockSpec(memory_space=pltpu.VMEM)
    anywhere = pl.BlockSpec(memory_space=pltpu.HBM)
    return pl.pallas_call(
        expert_kernel,
        out_shape=jax.ShapeDtypeStruct((slots * width // back, back), BF),
        in_specs=[vmem] + [anywhere] * 6,
        out_specs=vmem,
        scratch_shapes=[pltpu.VMEM(w.shape, BF) for w in weights] + [pltpu.SemaphoreType.DMA((6,))],
        compiler_params=pltpu.CompilerParams(vmem_limit_bytes=50 * 2**20),
        cost_estimate=pl.CostEstimate(
            flops=2 * slots * width * hidden * 10,
            bytes_accessed=12 * width * hidden,
            transcendentals=2 * slots * hidden,
        ),
        name="expert",
    )(rows, *weights)


def product_kernel(place_ref, *refs):
    contexts, tokens_ref, out_ref = refs[:-2], refs[-2], refs[-1]
    x_size, depth, cols = tokens_ref.shape
    z_size = len(contexts)
    tok = depth // z_size
    z_index, y_index, y_size = place_ref[0], place_ref[1], place_ref[2]
    total = None
    for step, ref in enumerate(contexts):
        at = pl.multiple_of(lax.rem(z_index + z_size - step, z_size) * tok, tok)
        tokens = tokens_ref[:, pl.ds(at, tok), :].reshape(x_size * tok, cols)
        term = dot_f32(ref[...], tokens)
        total = term if total is None else total + term
    heads = out_ref.shape[1]
    for step in range(out_ref.shape[0]):
        out_ref[lax.rem(y_index + y_size - step, y_size)] = total[step * heads:(step + 1) * heads].astype(BF)


def context_product(place, contexts, tokens_b, y_size):
    rows, depth = contexts[0].shape
    groups = len(contexts)
    cols = tokens_b.shape[2]
    return pl.pallas_call(
        product_kernel,
        out_shape=jax.ShapeDtypeStruct((y_size, rows // y_size, cols), BF),
        in_specs=[pl.BlockSpec(memory_space=pltpu.SMEM)] + [pl.BlockSpec(memory_space=pltpu.VMEM)] * (groups + 1),
        out_specs=pl.BlockSpec(memory_space=pltpu.VMEM),
        compiler_params=pltpu.CompilerParams(vmem_limit_bytes=16 * 2**20),
        cost_estimate=pl.CostEstimate(
            flops=2 * groups * rows * depth * cols, bytes_accessed=2 * groups * rows * depth, transcendentals=0
        ),
        name="context_product",
    )(place, *contexts, tokens_b)


def finish_kernel(mine_ref, came_ref, grad_ref, hidden_ref, columns_ref):
    parts, _, width = mine_ref.shape
    cols = columns_ref.shape[2]
    for i in range(parts):
        at = slice(i * width, (i + 1) * width)
        hidden = grad_ref[:, at].astype(F32) + (mine_ref[i] + came_ref[i])
        hidden_ref[:, at] = hidden
        for j in range(width // cols):
            columns_ref[i * (width // cols) + j] = hidden[:, j * cols:(j + 1) * cols].astype(BF)


def finish(mine, came, grad_half, groups):
    tok, width = grad_half.shape
    vmem = pl.BlockSpec(memory_space=pltpu.VMEM)
    return pl.pallas_call(
        finish_kernel,
        out_shape=(
            jax.ShapeDtypeStruct((tok, width), F32),
            jax.ShapeDtypeStruct((groups, tok, width // groups), BF),
        ),
        in_specs=[vmem] * 3,
        out_specs=(vmem, vmem),
        compiler_params=pltpu.CompilerParams(vmem_limit_bytes=8 * 2**20),
        cost_estimate=pl.CostEstimate(flops=3 * tok * width, bytes_accessed=16 * tok * width, transcendentals=0),
        name="finish",
    )(mine, came, grad_half)


def swap_pool(value):
    return lax.ppermute(value, "pool", ((0, 1), (1, 0)))


def exchange(value, axes):
    return lax.all_to_all(value, axes, split_axis=0, concat_axis=0, tiled=True)


def shifted(value, axis, size, step):
    return lax.ppermute(value, axis, tuple((s, (s + step) % size) for s in range(size)))


def spread_over_y(context_t, y_index, y_size):
    wide = context_t.shape[1] // y_size
    pieces = []
    for step in range(y_size):
        piece = lax.dynamic_slice_in_dim(context_t, lax.rem(y_index + step, y_size) * wide, wide, 1)
        pieces.append(shifted(piece, "y", y_size, step) if step else piece)
    return jnp.concatenate(pieces, axis=0)


def per_device(moe_in, out_grad, gates, routes, w_gate, w_up, w_down, context_t):
    tok_rows, model_width = moe_in.shape
    top_count = routes.shape[1]
    y_size, x_size, z_size = lax.axis_size("y"), lax.axis_size("x"), lax.axis_size("group")
    experts = y_size * x_size
    capacity = 2 * tok_rows * top_count // experts
    own_slots = capacity // 2
    pool_index = lax.axis_index("pool")
    y_index = lax.axis_index("y")
    half_width = model_width // 2
    pair_count = tok_rows * top_count

    expert_ids = routes.reshape(pair_count)
    hits = (expert_ids[:, None] == jnp.arange(experts, dtype=jnp.int32)[None, :]).astype(jnp.int32)
    earlier = jnp.cumsum(hits, axis=0) - hits
    position = jnp.sum(earlier * hits, axis=1)
    own = position // own_slots == pool_index
    slot_ids = jnp.where(own, expert_ids * own_slots + position % own_slots, -1)
    slot_ids = slot_ids.reshape(tok_rows, top_count)
    slot_grid = jnp.arange(experts * own_slots, dtype=jnp.int32)
    placed = slot_ids[:, :, None] == slot_grid[None, None, :]
    picker = jnp.any(placed, axis=1).astype(BF)
    weights = jnp.sum(jnp.where(placed, gates[:, :, None], 0.0), axis=1)

    piece_width = 2 * model_width * own_slots // ROWS
    parts = 2 * model_width // piece_width
    stacked = jnp.concatenate(
        [a[:, i * piece_width:(i + 1) * piece_width] for a in (moe_in, out_grad) for i in range(parts // 2)], 0
    )
    eye = jnp.eye(parts, dtype=BF)
    spread = (picker.T[:, None, None, :] * eye[None, :, :, None]).reshape(
        experts * ROWS, parts * tok_rows
    )
    send = dot_f32(spread, stacked).astype(BF).reshape(experts, ROWS, piece_width)
    send, context_t, weights = lax.optimization_barrier((send, context_t, weights))
    received = exchange(send, ("y", "x"))
    other_gate, other_up, other_down = swap_pool(w_gate[0]), swap_pool(w_up[0]), swap_pool(w_down[0])
    context_y = spread_over_y(context_t, y_index, y_size)
    received, context_y = lax.optimization_barrier((received, context_y))
    contexts = [shifted(context_y, "group", z_size, step) if step else context_y for step in range(z_size)]
    place = jnp.stack([lax.axis_index("group"), y_index, jnp.int32(y_size)]).astype(jnp.int32)

    back_width = model_width * own_slots // ROWS
    back_parts = model_width // back_width
    back = expert_rows(
        received.reshape(experts * ROWS, piece_width),
        (w_gate[0], w_up[0], w_down[0], other_gate, other_up, other_down),
        back_width,
    ).reshape(experts, ROWS, back_width)
    returned = exchange(back, ("y", "x"))
    returned, contexts[:6] = lax.optimization_barrier((returned, contexts[:6]))

    high = lax.reduce_precision(weights, 8, 7).astype(BF)
    low = (weights - high.astype(F32)).astype(BF)
    both = jnp.stack((high, low))
    back_eye = jnp.eye(back_parts, dtype=BF)
    mixer = (both[None, :, :, :, None] * back_eye[:, None, None, None, :]).reshape(
        back_parts * 2 * tok_rows, experts * ROWS
    )
    mixed = dot_f32(mixer, returned.reshape(experts * ROWS, back_width))
    mixed = jnp.sum(mixed.reshape(back_parts, 2, tok_rows, back_width), axis=1)
    per_half = back_parts // 2
    mine = lax.dynamic_slice_in_dim(mixed, pool_index * per_half, per_half, 0)
    theirs = lax.dynamic_slice_in_dim(mixed, (1 - pool_index) * per_half, per_half, 0)
    grad_half = lax.dynamic_slice_in_dim(out_grad, pool_index * half_width, half_width, 1)
    hidden_grad, by_column = finish(mine, swap_pool(theirs), grad_half, z_size)

    cols = half_width // z_size
    by_group = exchange(by_column, "group")
    gathered_b = exchange(
        jnp.broadcast_to(by_group[None], (x_size, z_size, tok_rows, cols)).reshape(
            x_size, z_size * tok_rows, cols
        ),
        "x",
    )
    partial_wo = context_product(place, contexts, gathered_b, y_size)
    terms = exchange(partial_wo, "y")
    wo_grad = jnp.sum(terms.astype(F32), axis=0)
    return (hidden_grad, wo_grad)


def solution(mesh):
    pool, group, ep = (mesh.shape[name] for name in ("pool", "group", "ep"))
    y_size = 8
    grid = Mesh(mesh.devices.reshape(pool, group, y_size, ep // y_size), ("pool", "group", "y", "x"))
    tokens = ("group", "y", "x")
    return jax.shard_map(
        per_device,
        mesh=grid,
        in_specs=(
            P(tokens, None),
            P(tokens, None),
            P(tokens, None),
            P(tokens, None),
            P(("y", "x"), None, "pool"),
            P(("y", "x"), None, "pool"),
            P(("y", "x"), "pool", None),
            P(("y", "x"), "group"),
        ),
        out_specs=(P(tokens, "pool"), P(("y", "x"), ("pool", "group"))),
        check_vma=False,
    )
```

```python
import jax
import jax.numpy as jnp
from jax import lax
from jax.experimental import pallas as pl
from jax.experimental.pallas import tpu as pltpu
from jax.sharding import Mesh, PartitionSpec as P

ROWS = 8
SORT = 256
BF = jnp.bfloat16
F32 = jnp.float32


def dot_f32(left, right):
    return jnp.dot(left, right, preferred_element_type=F32)


def dot_transposed(left, right):
    return lax.dot_general(left, right, (((1,), (1,)), ((), ())), preferred_element_type=F32)


def moved(rows_out, rows_in, source):
    at = lax.broadcasted_iota(jnp.int32, (rows_out, rows_in), 0)
    of = lax.broadcasted_iota(jnp.int32, (rows_out, rows_in), 1)
    return (of == source(at)).astype(BF)


def expert_kernel(rows_ref, *refs):
    weights, out_ref, held, sems = refs[:6], refs[6], refs[7:13], refs[13]
    copies = [pltpu.make_async_copy(w, h, sems.at[i]) for i, (w, h) in enumerate(zip(weights, held))]
    for copy in copies:
        copy.start()
    total_rows, piece = rows_ref.shape
    width = held[0].shape[0]
    parts = 2 * width // piece
    block = min(SORT, total_rows)
    slots = block // parts
    to_parts = moved(block, block, lambda i: lax.rem(i, slots) * parts + lax.div(i, slots))
    sorted_rows = [
        dot_f32(to_parts, rows_ref[i:i + block]).astype(BF) for i in range(0, total_rows, block)
    ]
    part = [
        jnp.concatenate([rows[i * slots:(i + 1) * slots] for rows in sorted_rows], axis=0)
        for i in range(parts)
    ]
    inputs_rows = jnp.concatenate(part[:parts // 2], axis=1)
    grads_rows = jnp.concatenate(part[parts // 2:], axis=1)
    total = None
    for half in range(2):
        gate_ref, up_ref, down_ref = held[3 * half:3 * half + 3]
        copies[3 * half].wait()
        gate_value = dot_f32(inputs_rows, gate_ref[...])
        copies[3 * half + 1].wait()
        up_value = dot_f32(inputs_rows, up_ref[...])
        copies[3 * half + 2].wait()
        act_grad = dot_transposed(grads_rows, down_ref[...])
        sigmoid_gate = jax.nn.sigmoid(gate_value)
        up_grad = (act_grad * gate_value * sigmoid_gate).astype(BF)
        gate_grad = (
            act_grad * up_value * sigmoid_gate * (1.0 + gate_value * (1.0 - sigmoid_gate))
        ).astype(BF)
        half_grad = dot_transposed(gate_grad, gate_ref[...]) + dot_transposed(up_grad, up_ref[...])
        total = half_grad if total is None else total + half_grad
    total = total.astype(BF)
    back = out_ref.shape[1]
    pieces = width // back
    block = min(SORT, out_ref.shape[0])
    slots = block // pieces
    to_slots = moved(block, block, lambda i: lax.rem(i, pieces) * slots + lax.div(i, pieces))
    for at in range(out_ref.shape[0] // block):
        rows = total[at * slots:(at + 1) * slots]
        stacked = jnp.concatenate([rows[:, i * back:(i + 1) * back] for i in range(pieces)], axis=0)
        out_ref[at * block:(at + 1) * block] = dot_f32(to_slots, stacked).astype(BF)


def expert_rows(rows, weights, back):
    width = weights[0].shape[0]
    slots = rows.size // (2 * width)
    hidden = weights[0].shape[1]
    vmem = pl.BlockSpec(memory_space=pltpu.VMEM)
    anywhere = pl.BlockSpec(memory_space=pltpu.HBM)
    return pl.pallas_call(
        expert_kernel,
        out_shape=jax.ShapeDtypeStruct((slots * width // back, back), BF),
        in_specs=[vmem] + [anywhere] * 6,
        out_specs=vmem,
        scratch_shapes=[pltpu.VMEM(w.shape, BF) for w in weights] + [pltpu.SemaphoreType.DMA((6,))],
        compiler_params=pltpu.CompilerParams(vmem_limit_bytes=50 * 2**20),
        cost_estimate=pl.CostEstimate(
            flops=2 * slots * width * hidden * 10,
            bytes_accessed=12 * width * hidden,
            transcendentals=2 * slots * hidden,
        ),
        name="expert",
    )(rows, *weights)


def product_kernel(place_ref, *refs):
    contexts, tokens_ref, out_ref = refs[:-2], refs[-2], refs[-1]
    x_size, depth, cols = tokens_ref.shape
    z_size = sum(ref.shape[0] for ref in contexts)
    tok = depth // z_size
    z_index, y_index = place_ref[0], place_ref[1]
    total = None
    for (ref, i), apart in zip(((ref, i) for ref in contexts for i in range(ref.shape[0])), doubled(z_size)):
        at = pl.multiple_of(jnp.bitwise_xor(z_index, apart) * tok, tok)
        tokens = tokens_ref[:, pl.ds(at, tok), :].reshape(x_size * tok, cols)
        term = dot_f32(ref[i], tokens)
        total = term if total is None else total + term
    heads = out_ref.shape[1]
    for apart in range(out_ref.shape[0]):
        out_ref[jnp.bitwise_xor(y_index, apart)] = total[apart * heads:(apart + 1) * heads].astype(BF)


def context_product(place, contexts, tokens_b, y_size):
    rows, depth = contexts[0].shape[1:]
    groups = sum(c.shape[0] for c in contexts)
    cols = tokens_b.shape[2]
    return pl.pallas_call(
        product_kernel,
        out_shape=jax.ShapeDtypeStruct((y_size, rows // y_size, cols), BF),
        in_specs=[pl.BlockSpec(memory_space=pltpu.SMEM)]
        + [pl.BlockSpec(memory_space=pltpu.VMEM)] * (len(contexts) + 1),
        out_specs=pl.BlockSpec(memory_space=pltpu.VMEM),
        compiler_params=pltpu.CompilerParams(vmem_limit_bytes=16 * 2**20),
        cost_estimate=pl.CostEstimate(
            flops=2 * groups * rows * depth * cols, bytes_accessed=2 * groups * rows * depth, transcendentals=0
        ),
        name="context_product",
    )(place, *contexts, tokens_b)


def finish_kernel(mine_ref, came_ref, grad_ref, hidden_ref, columns_ref):
    parts, _, width = mine_ref.shape
    cols = columns_ref.shape[2]
    for i in range(parts):
        at = slice(i * width, (i + 1) * width)
        hidden = grad_ref[:, at].astype(F32) + (mine_ref[i] + came_ref[i])
        hidden_ref[:, at] = hidden
        for j in range(width // cols):
            columns_ref[i * (width // cols) + j] = hidden[:, j * cols:(j + 1) * cols].astype(BF)


def finish(mine, came, grad_half, groups):
    tok, width = grad_half.shape
    vmem = pl.BlockSpec(memory_space=pltpu.VMEM)
    return pl.pallas_call(
        finish_kernel,
        out_shape=(
            jax.ShapeDtypeStruct((tok, width), F32),
            jax.ShapeDtypeStruct((groups, tok, width // groups), BF),
        ),
        in_specs=[vmem] * 3,
        out_specs=(vmem, vmem),
        compiler_params=pltpu.CompilerParams(vmem_limit_bytes=8 * 2**20),
        cost_estimate=pl.CostEstimate(flops=3 * tok * width, bytes_accessed=16 * tok * width, transcendentals=0),
        name="finish",
    )(mine, came, grad_half)


def swap_pool(value):
    return lax.ppermute(value, "pool", ((0, 1), (1, 0)))


def exchange(value, axes):
    return lax.all_to_all(value, axes, split_axis=0, concat_axis=0, tiled=True)


def swapped(value, axis, size, bit):
    return lax.ppermute(value, axis, tuple((s, s ^ bit) for s in range(size)))


def spread_over_y(context_t, y_index, y_size):
    wide = context_t.shape[1] // y_size
    places = [
        lax.dynamic_slice_in_dim(context_t, jnp.bitwise_xor(y_index, r) * wide, wide, 1)
        for r in range(y_size)
    ]
    bit = 1
    while bit < y_size:
        crossing = [r for r in range(y_size) if r & bit]
        came = swapped(jnp.stack([places[r] for r in crossing]), "y", y_size, bit)
        for i, r in enumerate(crossing):
            places[r] = came[i]
        bit *= 2
    return jnp.concatenate(places, axis=0)[None]


def doubled(size):
    order, bit = [0], size // 2
    while bit:
        order += [r ^ bit for r in order]
        bit //= 2
    return order


def per_device(moe_in, out_grad, gates, routes, w_gate, w_up, w_down, context_t):
    tok_rows, model_width = moe_in.shape
    top_count = routes.shape[1]
    y_size, x_size, z_size = lax.axis_size("y"), lax.axis_size("x"), lax.axis_size("group")
    experts = y_size * x_size
    capacity = 2 * tok_rows * top_count // experts
    own_slots = capacity // 2
    pool_index = lax.axis_index("pool")
    y_index = lax.axis_index("y")
    half_width = model_width // 2
    pair_count = tok_rows * top_count

    expert_ids = routes.reshape(pair_count)
    hits = (expert_ids[:, None] == jnp.arange(experts, dtype=jnp.int32)[None, :]).astype(jnp.int32)
    earlier = jnp.cumsum(hits, axis=0) - hits
    position = jnp.sum(earlier * hits, axis=1)
    own = position // own_slots == pool_index
    slot_ids = jnp.where(own, expert_ids * own_slots + position % own_slots, -1)
    slot_ids = slot_ids.reshape(tok_rows, top_count)
    slot_grid = jnp.arange(experts * own_slots, dtype=jnp.int32)
    placed = slot_ids[:, :, None] == slot_grid[None, None, :]
    picker = jnp.any(placed, axis=1).astype(BF)
    weights = jnp.sum(jnp.where(placed, gates[:, :, None], 0.0), axis=1)

    piece_width = 2 * model_width * own_slots // ROWS
    parts = 2 * model_width // piece_width
    stacked = jnp.concatenate(
        [a[:, i * piece_width:(i + 1) * piece_width] for a in (moe_in, out_grad) for i in range(parts // 2)], 0
    )
    eye = jnp.eye(parts, dtype=BF)
    spread = (picker.T[:, None, None, :] * eye[None, :, :, None]).reshape(
        experts * ROWS, parts * tok_rows
    )
    send = dot_f32(spread, stacked).astype(BF).reshape(experts, ROWS, piece_width)
    context_y = spread_over_y(context_t, y_index, y_size)
    send, weights, context_y = lax.optimization_barrier((send, weights, context_y))
    received = exchange(send, ("y", "x"))
    contexts, bit = [context_y, swapped(context_y, "group", z_size, z_size // 2)], z_size // 4
    other_gate = swap_pool(w_gate[0])
    up_matrix, down_matrix, contexts = lax.optimization_barrier((w_up[0], w_down[0], contexts))
    other_up, other_down = swap_pool(up_matrix), swap_pool(down_matrix)
    while bit:
        contexts.append(swapped(jnp.concatenate(contexts, axis=0), "group", z_size, bit))
        if bit > 1:
            received, contexts = lax.optimization_barrier((received, contexts))
        bit //= 2
    place = jnp.stack([lax.axis_index("group"), y_index]).astype(jnp.int32)

    back_width = model_width * own_slots // ROWS
    back_parts = model_width // back_width
    back = expert_rows(
        received.reshape(experts * ROWS, piece_width),
        (w_gate[0], w_up[0], w_down[0], other_gate, other_up, other_down),
        back_width,
    ).reshape(experts, ROWS, back_width)
    returned = exchange(back, ("y", "x"))
    returned, contexts = lax.optimization_barrier((returned, contexts))

    high = lax.reduce_precision(weights, 8, 7).astype(BF)
    low = (weights - high.astype(F32)).astype(BF)
    both = jnp.stack((high, low))
    back_eye = jnp.eye(back_parts, dtype=BF)
    mixer = (both[None, :, :, :, None] * back_eye[:, None, None, None, :]).reshape(
        back_parts * 2 * tok_rows, experts * ROWS
    )
    mixed = dot_f32(mixer, returned.reshape(experts * ROWS, back_width))
    mixed = jnp.sum(mixed.reshape(back_parts, 2, tok_rows, back_width), axis=1)
    per_half = back_parts // 2
    mine = lax.dynamic_slice_in_dim(mixed, pool_index * per_half, per_half, 0)
    theirs = lax.dynamic_slice_in_dim(mixed, (1 - pool_index) * per_half, per_half, 0)
    grad_half = lax.dynamic_slice_in_dim(out_grad, pool_index * half_width, half_width, 1)
    hidden_grad, by_column = finish(mine, swap_pool(theirs), grad_half, z_size)

    cols = half_width // z_size
    by_group = exchange(by_column, "group")
    gathered_b = exchange(
        jnp.broadcast_to(by_group[None], (x_size, z_size, tok_rows, cols)).reshape(
            x_size, z_size * tok_rows, cols
        ),
        "x",
    )
    partial_wo = context_product(place, contexts, gathered_b, y_size)
    terms = exchange(partial_wo, "y")
    wo_grad = jnp.sum(terms.astype(F32), axis=0)
    return (hidden_grad, wo_grad)


def solution(mesh):
    pool, group, ep = (mesh.shape[name] for name in ("pool", "group", "ep"))
    y_size = 8
    grid = Mesh(mesh.devices.reshape(pool, group, y_size, ep // y_size), ("pool", "group", "y", "x"))
    tokens = ("group", "y", "x")
    return jax.shard_map(
        per_device,
        mesh=grid,
        in_specs=(
            P(tokens, None),
            P(tokens, None),
            P(tokens, None),
            P(tokens, None),
            P(("y", "x"), None, "pool"),
            P(("y", "x"), None, "pool"),
            P(("y", "x"), "pool", None),
            P(("y", "x"), "group"),
        ),
        out_specs=(P(tokens, "pool"), P(("y", "x"), ("pool", "group"))),
        check_vma=False,
    )
```

```python
import jax
import jax.numpy as jnp
from jax import lax
from jax.experimental import pallas as pl
from jax.experimental.pallas import tpu as pltpu
from jax.sharding import Mesh, PartitionSpec as P

ROWS = 8
SORT = 256
Z_BLOCKS = 4
BF = jnp.bfloat16
F32 = jnp.float32


def dot_f32(left, right):
    return jnp.dot(left, right, preferred_element_type=F32)


def dot_transposed(left, right):
    return lax.dot_general(left, right, (((1,), (1,)), ((), ())), preferred_element_type=F32)


def moved(rows_out, rows_in, source):
    at = lax.broadcasted_iota(jnp.int32, (rows_out, rows_in), 0)
    of = lax.broadcasted_iota(jnp.int32, (rows_out, rows_in), 1)
    return (of == source(at)).astype(BF)


def expert_kernel(rows_ref, *refs):
    weights, out_ref, held, sems = refs[:6], refs[6], refs[7:13], refs[13]
    copies = [pltpu.make_async_copy(w, h, sems.at[i]) for i, (w, h) in enumerate(zip(weights, held))]
    for copy in copies:
        copy.start()
    total_rows, piece = rows_ref.shape
    width = held[0].shape[0]
    parts = 2 * width // piece
    block = min(SORT, total_rows)
    slots = block // parts
    to_parts = moved(block, block, lambda i: lax.rem(i, slots) * parts + lax.div(i, slots))
    sorted_rows = [
        dot_f32(to_parts, rows_ref[i:i + block]).astype(BF) for i in range(0, total_rows, block)
    ]
    part = [
        jnp.concatenate([rows[i * slots:(i + 1) * slots] for rows in sorted_rows], axis=0)
        for i in range(parts)
    ]
    inputs_rows = jnp.concatenate(part[:parts // 2], axis=1)
    grads_rows = jnp.concatenate(part[parts // 2:], axis=1)
    total = None
    for half in range(2):
        gate_ref, up_ref, down_ref = held[3 * half:3 * half + 3]
        copies[3 * half].wait()
        gate_value = dot_f32(inputs_rows, gate_ref[...])
        copies[3 * half + 1].wait()
        up_value = dot_f32(inputs_rows, up_ref[...])
        copies[3 * half + 2].wait()
        act_grad = dot_transposed(grads_rows, down_ref[...])
        sigmoid_gate = jax.nn.sigmoid(gate_value)
        up_grad = (act_grad * gate_value * sigmoid_gate).astype(BF)
        gate_grad = (
            act_grad * up_value * sigmoid_gate * (1.0 + gate_value * (1.0 - sigmoid_gate))
        ).astype(BF)
        half_grad = dot_transposed(gate_grad, gate_ref[...]) + dot_transposed(up_grad, up_ref[...])
        total = half_grad if total is None else total + half_grad
    total = total.astype(BF)
    back = out_ref.shape[1]
    pieces = width // back
    block = min(SORT, out_ref.shape[0])
    slots = block // pieces
    to_slots = moved(block, block, lambda i: lax.rem(i, pieces) * slots + lax.div(i, pieces))
    for at in range(out_ref.shape[0] // block):
        rows = total[at * slots:(at + 1) * slots]
        stacked = jnp.concatenate([rows[:, i * back:(i + 1) * back] for i in range(pieces)], axis=0)
        out_ref[at * block:(at + 1) * block] = dot_f32(to_slots, stacked).astype(BF)


def expert_rows(rows, weights, back):
    width = weights[0].shape[0]
    slots = rows.size // (2 * width)
    hidden = weights[0].shape[1]
    vmem = pl.BlockSpec(memory_space=pltpu.VMEM)
    anywhere = pl.BlockSpec(memory_space=pltpu.HBM)
    return pl.pallas_call(
        expert_kernel,
        out_shape=jax.ShapeDtypeStruct((slots * width // back, back), BF),
        in_specs=[vmem] + [anywhere] * 6,
        out_specs=vmem,
        scratch_shapes=[pltpu.VMEM(w.shape, BF) for w in weights] + [pltpu.SemaphoreType.DMA((6,))],
        compiler_params=pltpu.CompilerParams(vmem_limit_bytes=50 * 2**20),
        cost_estimate=pl.CostEstimate(
            flops=2 * slots * width * hidden * 10,
            bytes_accessed=12 * width * hidden,
            transcendentals=2 * slots * hidden,
        ),
        name="expert",
    )(rows, *weights)


def product_kernel(place_ref, *refs):
    contexts, tokens_ref, out_ref = refs[:-2], refs[-2], refs[-1]
    peers, depth, width = tokens_ref.shape
    tok = depth // len(contexts)
    total = None
    for i, ref in enumerate(contexts):
        tokens = tokens_ref[:, i * tok:(i + 1) * tok, :].reshape(peers * tok, width)
        term = dot_f32(ref[...], tokens)
        total = term if total is None else total + term
    blocks, heads, cols = out_ref.shape
    z_blocks = width // cols
    y_blocks = blocks // z_blocks
    yh_index = place_ref[0]
    for z in range(z_blocks):
        for apart in range(y_blocks):
            out_ref[z * y_blocks + jnp.bitwise_xor(yh_index, apart)] = total[
                apart * heads:(apart + 1) * heads, z * cols:(z + 1) * cols
            ].astype(BF)


def context_product(yh_index, contexts, tokens_b, y_blocks, z_blocks):
    rows, depth = contexts[0].shape
    width = tokens_b.shape[2]
    return pl.pallas_call(
        product_kernel,
        out_shape=jax.ShapeDtypeStruct((z_blocks * y_blocks, rows // y_blocks, width // z_blocks), BF),
        in_specs=[pl.BlockSpec(memory_space=pltpu.SMEM)]
        + [pl.BlockSpec(memory_space=pltpu.VMEM)] * (len(contexts) + 1),
        out_specs=pl.BlockSpec(memory_space=pltpu.VMEM),
        compiler_params=pltpu.CompilerParams(vmem_limit_bytes=16 * 2**20),
        cost_estimate=pl.CostEstimate(
            flops=2 * len(contexts) * rows * depth * width,
            bytes_accessed=2 * len(contexts) * depth * (rows + width),
            transcendentals=0,
        ),
        name="context_product",
    )(yh_index.astype(jnp.int32).reshape(1), *contexts, tokens_b)


def finish_kernel(zl_ref, mine_ref, came_ref, grad_ref, hidden_ref, keep_ref, send_ref):
    parts, _, width = mine_ref.shape
    for i in range(parts):
        at = slice(i * width, (i + 1) * width)
        hidden_ref[:, at] = grad_ref[:, at].astype(F32) + (mine_ref[i] + came_ref[i])
    first = zl_ref[0] == 0
    cols = hidden_ref.shape[1] // (2 * Z_BLOCKS)
    for z in range(Z_BLOCKS):
        even = hidden_ref[:, 2 * z * cols:(2 * z + 1) * cols]
        odd = hidden_ref[:, (2 * z + 1) * cols:(2 * z + 2) * cols]
        at = slice(z * cols, (z + 1) * cols)
        keep_ref[:, at] = jnp.where(first, even, odd).astype(BF)
        send_ref[:, at] = jnp.where(first, odd, even).astype(BF)


def finish(zl_index, mine, came, grad_half):
    tok, width = grad_half.shape
    vmem = pl.BlockSpec(memory_space=pltpu.VMEM)
    half = jax.ShapeDtypeStruct((tok, width // 2), BF)
    return pl.pallas_call(
        finish_kernel,
        out_shape=(jax.ShapeDtypeStruct((tok, width), F32), half, half),
        in_specs=[pl.BlockSpec(memory_space=pltpu.SMEM)] + [vmem] * 3,
        out_specs=(vmem,) * 3,
        compiler_params=pltpu.CompilerParams(vmem_limit_bytes=8 * 2**20),
        cost_estimate=pl.CostEstimate(flops=3 * tok * width, bytes_accessed=16 * tok * width, transcendentals=0),
        name="finish",
    )(zl_index.astype(jnp.int32).reshape(1), mine, came, grad_half)


def swap_pool(value):
    return lax.ppermute(value, "pool", ((0, 1), (1, 0)))


def exchange(value, axes):
    return lax.all_to_all(value, axes, split_axis=0, concat_axis=0, tiled=True)


def swapped(value, axis, size, bit):
    return lax.ppermute(value, axis, tuple((s, s ^ bit) for s in range(size)))


def spread_over_yh(context_t, yh_index, y_blocks, others):
    wide = context_t.shape[1] // y_blocks
    places = [
        lax.dynamic_slice_in_dim(context_t, jnp.bitwise_xor(yh_index, r) * wide, wide, 1)
        for r in range(y_blocks)
    ]
    bit = 1
    while bit < y_blocks:
        crossing = [r for r in range(y_blocks) if r & bit]
        came = swapped(jnp.concatenate([places[r] for r in crossing], axis=0), "yh", y_blocks, bit)
        if bit == 1:
            came, others = lax.optimization_barrier((came, others))
        heads = context_t.shape[0]
        for i, r in enumerate(crossing):
            places[r] = came[i * heads:(i + 1) * heads]
        bit *= 2
    return jnp.concatenate(places, axis=0), others


def per_device(moe_in, out_grad, gates, routes, w_gate, w_up, w_down, context_t):
    tok_rows, model_width = moe_in.shape
    top_count = routes.shape[1]
    plane = ("yh", "yl", "x")
    experts = lax.axis_size(plane)
    y_blocks, z_blocks = lax.axis_size("yh"), lax.axis_size("zh")
    peers = experts // y_blocks
    capacity = 2 * tok_rows * top_count // experts
    own_slots = capacity // 2
    pool_index = lax.axis_index("pool")
    yh_index, zl_index = lax.axis_index("yh"), lax.axis_index("zl")
    half_width = model_width // 2
    pair_count = tok_rows * top_count

    expert_ids = routes.reshape(pair_count)
    hits = (expert_ids[:, None] == jnp.arange(experts, dtype=jnp.int32)[None, :]).astype(jnp.int32)
    earlier = jnp.cumsum(hits, axis=0) - hits
    position = jnp.sum(earlier * hits, axis=1)
    own = position // own_slots == pool_index
    slot_ids = jnp.where(own, expert_ids * own_slots + position % own_slots, -1)
    slot_ids = slot_ids.reshape(tok_rows, top_count)
    slot_grid = jnp.arange(experts * own_slots, dtype=jnp.int32)
    placed = slot_ids[:, :, None] == slot_grid[None, None, :]
    picker = jnp.any(placed, axis=1).astype(BF)
    weights = jnp.sum(jnp.where(placed, gates[:, :, None], 0.0), axis=1)

    piece_width = 2 * model_width * own_slots // ROWS
    parts = 2 * model_width // piece_width
    stacked = jnp.concatenate(
        [a[:, i * piece_width:(i + 1) * piece_width] for a in (moe_in, out_grad) for i in range(parts // 2)], 0
    )
    eye = jnp.eye(parts, dtype=BF)
    spread = (picker.T[:, None, None, :] * eye[None, :, :, None]).reshape(
        experts * ROWS, parts * tok_rows
    )
    send = dot_f32(spread, stacked).astype(BF).reshape(experts, ROWS, piece_width)
    send, weights, context_t = lax.optimization_barrier((send, weights, context_t))
    received = exchange(send, plane)
    other_gate = swap_pool(w_gate[0])
    context_y, (up_matrix, down_matrix) = spread_over_yh(context_t, yh_index, y_blocks, (w_up[0], w_down[0]))
    other_up, other_down = swap_pool(up_matrix), swap_pool(down_matrix)
    received, context_y = lax.optimization_barrier((received, context_y))

    back_width = model_width * own_slots // ROWS
    back_parts = model_width // back_width
    back = expert_rows(
        received.reshape(experts * ROWS, piece_width),
        (w_gate[0], w_up[0], w_down[0], other_gate, other_up, other_down),
        back_width,
    ).reshape(experts, ROWS, back_width)
    returned = exchange(back, plane)
    contexts = [context_y, swapped(context_y, "zl", 2, 1)]
    returned, contexts = lax.optimization_barrier((returned, contexts))

    high = lax.reduce_precision(weights, 8, 7).astype(BF)
    low = (weights - high.astype(F32)).astype(BF)
    both = jnp.stack((high, low))
    back_eye = jnp.eye(back_parts, dtype=BF)
    mixer = (both[None, :, :, :, None] * back_eye[:, None, None, None, :]).reshape(
        back_parts * 2 * tok_rows, experts * ROWS
    )
    mixed = dot_f32(mixer, returned.reshape(experts * ROWS, back_width))
    mixed = jnp.sum(mixed.reshape(back_parts, 2, tok_rows, back_width), axis=1)
    per_half = back_parts // 2
    mine = lax.dynamic_slice_in_dim(mixed, pool_index * per_half, per_half, 0)
    theirs = lax.dynamic_slice_in_dim(mixed, (1 - pool_index) * per_half, per_half, 0)
    grad_half = lax.dynamic_slice_in_dim(out_grad, pool_index * half_width, half_width, 1)
    hidden_grad, keep, give = finish(zl_index, mine, swap_pool(theirs), grad_half)
    pair = jnp.concatenate((keep, swapped(give, "zl", 2, 1)), axis=0)
    gathered_b = exchange(jnp.broadcast_to(pair[None], (peers, *pair.shape)), ("yl", "x"))
    terms = exchange(
        context_product(yh_index, contexts, gathered_b, y_blocks, z_blocks), ("zh", "yh")
    )
    wo_grad = jnp.sum(terms.astype(F32), axis=0)
    return (hidden_grad, wo_grad)


def solution(mesh):
    pool, group, ep = (mesh.shape[name] for name in ("pool", "group", "ep"))
    y_blocks, x_size = 4, 8
    grid = Mesh(
        mesh.devices.reshape(pool, Z_BLOCKS, group // Z_BLOCKS, y_blocks, ep // (y_blocks * x_size), x_size),
        ("pool", "zh", "zl", "yh", "yl", "x"),
    )
    group, plane = ("zh", "zl"), ("yh", "yl", "x")
    tokens = group + plane
    return jax.shard_map(
        per_device,
        mesh=grid,
        in_specs=(
            P(tokens, None),
            P(tokens, None),
            P(tokens, None),
            P(tokens, None),
            P(plane, None, "pool"),
            P(plane, None, "pool"),
            P(plane, "pool", None),
            P(plane, group),
        ),
        out_specs=(P(tokens, "pool"), P(plane, ("pool",) + group)),
        check_vma=False,
    )
```

```python
import jax
import jax.numpy as jnp
from jax import lax
from jax.experimental import pallas as pl
from jax.experimental.pallas import tpu as pltpu
from jax.sharding import Mesh, PartitionSpec as P

ROWS = 8
SORT = 256
Z_BLOCKS = 4
BF = jnp.bfloat16
F32 = jnp.float32


def dot_f32(left, right):
    return jnp.dot(left, right, preferred_element_type=F32)


def dot_transposed(left, right):
    return lax.dot_general(left, right, (((1,), (1,)), ((), ())), preferred_element_type=F32)


def moved(rows_out, rows_in, source):
    at = lax.broadcasted_iota(jnp.int32, (rows_out, rows_in), 0)
    of = lax.broadcasted_iota(jnp.int32, (rows_out, rows_in), 1)
    return (of == source(at)).astype(BF)


def expert_kernel(rows_ref, *refs):
    weights, out_ref, held, sems = refs[:6], refs[6], refs[7:13], refs[13]
    copies = [pltpu.make_async_copy(w, h, sems.at[i]) for i, (w, h) in enumerate(zip(weights, held))]
    for copy in copies:
        copy.start()
    total_rows, piece = rows_ref.shape
    width = held[0].shape[0]
    parts = 2 * width // piece
    block = min(SORT, total_rows)
    slots = block // parts
    to_parts = moved(block, block, lambda i: lax.rem(i, slots) * parts + lax.div(i, slots))
    sorted_rows = [
        dot_f32(to_parts, rows_ref[i:i + block]).astype(BF) for i in range(0, total_rows, block)
    ]
    part = [
        jnp.concatenate([rows[i * slots:(i + 1) * slots] for rows in sorted_rows], axis=0)
        for i in range(parts)
    ]
    inputs_rows = jnp.concatenate(part[:parts // 2], axis=1)
    grads_rows = jnp.concatenate(part[parts // 2:], axis=1)
    total = None
    for half in range(2):
        gate_ref, up_ref, down_ref = held[3 * half:3 * half + 3]
        copies[3 * half].wait()
        gate_value = dot_f32(inputs_rows, gate_ref[...])
        copies[3 * half + 1].wait()
        up_value = dot_f32(inputs_rows, up_ref[...])
        copies[3 * half + 2].wait()
        act_grad = dot_transposed(grads_rows, down_ref[...])
        sigmoid_gate = jax.nn.sigmoid(gate_value)
        up_grad = (act_grad * gate_value * sigmoid_gate).astype(BF)
        gate_grad = (
            act_grad * up_value * sigmoid_gate * (1.0 + gate_value * (1.0 - sigmoid_gate))
        ).astype(BF)
        half_grad = dot_transposed(gate_grad, gate_ref[...]) + dot_transposed(up_grad, up_ref[...])
        total = half_grad if total is None else total + half_grad
    total = total.astype(BF)
    back = out_ref.shape[1]
    pieces = width // back
    block = min(SORT, out_ref.shape[0])
    slots = block // pieces
    to_slots = moved(block, block, lambda i: lax.rem(i, pieces) * slots + lax.div(i, pieces))
    for at in range(out_ref.shape[0] // block):
        rows = total[at * slots:(at + 1) * slots]
        stacked = jnp.concatenate([rows[:, i * back:(i + 1) * back] for i in range(pieces)], axis=0)
        out_ref[at * block:(at + 1) * block] = dot_f32(to_slots, stacked).astype(BF)


def expert_rows(rows, weights, back):
    width = weights[0].shape[0]
    slots = rows.size // (2 * width)
    hidden = weights[0].shape[1]
    vmem = pl.BlockSpec(memory_space=pltpu.VMEM)
    anywhere = pl.BlockSpec(memory_space=pltpu.HBM)
    return pl.pallas_call(
        expert_kernel,
        out_shape=jax.ShapeDtypeStruct((slots * width // back, back), BF),
        in_specs=[vmem] + [anywhere] * 6,
        out_specs=vmem,
        scratch_shapes=[pltpu.VMEM(w.shape, BF) for w in weights] + [pltpu.SemaphoreType.DMA((6,))],
        compiler_params=pltpu.CompilerParams(vmem_limit_bytes=50 * 2**20),
        cost_estimate=pl.CostEstimate(
            flops=2 * slots * width * hidden * 10,
            bytes_accessed=12 * width * hidden,
            transcendentals=2 * slots * hidden,
        ),
        name="expert",
    )(rows, *weights)


def product_kernel(place_ref, *refs):
    contexts, tokens_ref, out_ref = refs[:-2], refs[-2], refs[-1]
    peers, depth, width = tokens_ref.shape
    tok = depth // len(contexts)
    total = None
    for i, ref in enumerate(contexts):
        tokens = tokens_ref[:, i * tok:(i + 1) * tok, :].reshape(peers * tok, width)
        term = dot_f32(ref[...], tokens)
        total = term if total is None else total + term
    blocks, heads, cols = out_ref.shape
    z_blocks = width // cols
    y_blocks = blocks // z_blocks
    yh_index = place_ref[0]
    for z in range(z_blocks):
        for apart in range(y_blocks):
            out_ref[z * y_blocks + jnp.bitwise_xor(yh_index, apart)] = total[
                apart * heads:(apart + 1) * heads, z * cols:(z + 1) * cols
            ].astype(BF)


def context_product(yh_index, contexts, tokens_b, y_blocks, z_blocks):
    rows, depth = contexts[0].shape
    width = tokens_b.shape[2]
    return pl.pallas_call(
        product_kernel,
        out_shape=jax.ShapeDtypeStruct((z_blocks * y_blocks, rows // y_blocks, width // z_blocks), BF),
        in_specs=[pl.BlockSpec(memory_space=pltpu.SMEM)]
        + [pl.BlockSpec(memory_space=pltpu.VMEM)] * (len(contexts) + 1),
        out_specs=pl.BlockSpec(memory_space=pltpu.VMEM),
        compiler_params=pltpu.CompilerParams(vmem_limit_bytes=16 * 2**20),
        cost_estimate=pl.CostEstimate(
            flops=2 * len(contexts) * rows * depth * width,
            bytes_accessed=2 * len(contexts) * depth * (rows + width),
            transcendentals=0,
        ),
        name="context_product",
    )(yh_index.astype(jnp.int32).reshape(1), *contexts, tokens_b)


def finish_kernel(zl_ref, mine_ref, came_ref, grad_ref, hidden_ref, keep_ref, send_ref):
    parts, _, width = mine_ref.shape
    for i in range(parts):
        at = slice(i * width, (i + 1) * width)
        hidden_ref[:, at] = grad_ref[:, at].astype(F32) + (mine_ref[i] + came_ref[i])
    first = zl_ref[0] == 0
    cols = hidden_ref.shape[1] // (2 * Z_BLOCKS)
    for z in range(Z_BLOCKS):
        even = hidden_ref[:, 2 * z * cols:(2 * z + 1) * cols]
        odd = hidden_ref[:, (2 * z + 1) * cols:(2 * z + 2) * cols]
        at = slice(z * cols, (z + 1) * cols)
        keep_ref[:, at] = jnp.where(first, even, odd).astype(BF)
        send_ref[:, at] = jnp.where(first, odd, even).astype(BF)


def finish(zl_index, mine, came, grad_half):
    tok, width = grad_half.shape
    vmem = pl.BlockSpec(memory_space=pltpu.VMEM)
    half = jax.ShapeDtypeStruct((tok, width // 2), BF)
    return pl.pallas_call(
        finish_kernel,
        out_shape=(jax.ShapeDtypeStruct((tok, width), F32), half, half),
        in_specs=[pl.BlockSpec(memory_space=pltpu.SMEM)] + [vmem] * 3,
        out_specs=(vmem,) * 3,
        compiler_params=pltpu.CompilerParams(vmem_limit_bytes=8 * 2**20),
        cost_estimate=pl.CostEstimate(flops=3 * tok * width, bytes_accessed=16 * tok * width, transcendentals=0),
        name="finish",
    )(zl_index.astype(jnp.int32).reshape(1), mine, came, grad_half)


def swap_pool(value):
    return lax.ppermute(value, "pool", ((0, 1), (1, 0)))


def exchange(value, axes):
    return lax.all_to_all(value, axes, split_axis=0, concat_axis=0, tiled=True)


def swapped(value, axis, size, bit):
    return lax.ppermute(value, axis, tuple((s, s ^ bit) for s in range(size)))


def spread_over_yh(context_t, yh_index, y_blocks):
    wide, heads = context_t.shape[1] // y_blocks, context_t.shape[0]
    places = [
        lax.dynamic_slice_in_dim(context_t, jnp.bitwise_xor(yh_index, r) * wide, wide, 1)
        for r in range(y_blocks)
    ]
    bit = 1
    while bit < y_blocks:
        crossing = [r for r in range(y_blocks) if r & bit]
        came = swapped(jnp.concatenate([places[r] for r in crossing], axis=0), "yh", y_blocks, bit)
        places = list(places)
        for i, r in enumerate(crossing):
            places[r] = came[i * heads:(i + 1) * heads]
        places = yield places
        bit *= 2


def per_device(moe_in, out_grad, gates, routes, w_gate, w_up, w_down, context_t):
    tok_rows, model_width = moe_in.shape
    top_count = routes.shape[1]
    plane = ("yh", "yl", "x")
    experts = lax.axis_size(plane)
    y_blocks, z_blocks = lax.axis_size("yh"), lax.axis_size("zh")
    peers = experts // y_blocks
    capacity = 2 * tok_rows * top_count // experts
    own_slots = capacity // 2
    pool_index = lax.axis_index("pool")
    yh_index, zl_index = lax.axis_index("yh"), lax.axis_index("zl")
    half_width = model_width // 2
    pair_count = tok_rows * top_count

    expert_ids = routes.reshape(pair_count)
    hits = (expert_ids[:, None] == jnp.arange(experts, dtype=jnp.int32)[None, :]).astype(jnp.int32)
    earlier = jnp.cumsum(hits, axis=0) - hits
    position = jnp.sum(earlier * hits, axis=1)
    own = position // own_slots == pool_index
    slot_ids = jnp.where(own, expert_ids * own_slots + position % own_slots, -1)
    slot_ids = slot_ids.reshape(tok_rows, top_count)
    slot_grid = jnp.arange(experts * own_slots, dtype=jnp.int32)
    placed = slot_ids[:, :, None] == slot_grid[None, None, :]
    picker = jnp.any(placed, axis=1).astype(BF)
    weights = jnp.sum(jnp.where(placed, gates[:, :, None], 0.0), axis=1)

    piece_width = 2 * model_width * own_slots // ROWS
    parts = 2 * model_width // piece_width
    stacked = jnp.concatenate(
        [a[:, i * piece_width:(i + 1) * piece_width] for a in (moe_in, out_grad) for i in range(parts // 2)], 0
    )
    eye = jnp.eye(parts, dtype=BF)
    spread = (picker.T[:, None, None, :] * eye[None, :, :, None]).reshape(
        experts * ROWS, parts * tok_rows
    )
    send = dot_f32(spread, stacked).astype(BF).reshape(experts, ROWS, piece_width)
    swaps = spread_over_yh(context_t, yh_index, y_blocks)
    places = next(swaps)
    send, weights, places = lax.optimization_barrier((send, weights, places))
    received = exchange(send, plane)
    other_gate, other_up, other_down = swap_pool(w_gate[0]), swap_pool(w_up[0]), swap_pool(w_down[0])
    try:
        while True:
            places = swaps.send(places)
    except StopIteration:
        context_y = jnp.concatenate(places, axis=0)
    received, context_y = lax.optimization_barrier((received, context_y))

    back_width = model_width * own_slots // ROWS
    back_parts = model_width // back_width
    back = expert_rows(
        received.reshape(experts * ROWS, piece_width),
        (w_gate[0], w_up[0], w_down[0], other_gate, other_up, other_down),
        back_width,
    ).reshape(experts, ROWS, back_width)
    returned = exchange(back, plane)
    contexts = [context_y, swapped(context_y, "zl", 2, 1)]
    returned, contexts = lax.optimization_barrier((returned, contexts))

    high = lax.reduce_precision(weights, 8, 7).astype(BF)
    low = (weights - high.astype(F32)).astype(BF)
    both = jnp.stack((high, low))
    back_eye = jnp.eye(back_parts, dtype=BF)
    mixer = (both[None, :, :, :, None] * back_eye[:, None, None, None, :]).reshape(
        back_parts * 2 * tok_rows, experts * ROWS
    )
    mixed = dot_f32(mixer, returned.reshape(experts * ROWS, back_width))
    mixed = jnp.sum(mixed.reshape(back_parts, 2, tok_rows, back_width), axis=1)
    per_half = back_parts // 2
    mine = lax.dynamic_slice_in_dim(mixed, pool_index * per_half, per_half, 0)
    theirs = lax.dynamic_slice_in_dim(mixed, (1 - pool_index) * per_half, per_half, 0)
    grad_half = lax.dynamic_slice_in_dim(out_grad, pool_index * half_width, half_width, 1)
    hidden_grad, keep, give = finish(zl_index, mine, swap_pool(theirs), grad_half)
    pair = jnp.concatenate((keep, swapped(give, "zl", 2, 1)), axis=0)
    gathered_b = exchange(jnp.broadcast_to(pair[None], (peers, *pair.shape)), ("yl", "x"))
    terms = exchange(
        context_product(yh_index, contexts, gathered_b, y_blocks, z_blocks), ("zh", "yh")
    )
    wo_grad = jnp.sum(terms.astype(F32), axis=0)
    return (hidden_grad, wo_grad)


def solution(mesh):
    pool, group, ep = (mesh.shape[name] for name in ("pool", "group", "ep"))
    y_blocks, x_size = 4, 8
    grid = Mesh(
        mesh.devices.reshape(pool, Z_BLOCKS, group // Z_BLOCKS, y_blocks, ep // (y_blocks * x_size), x_size),
        ("pool", "zh", "zl", "yh", "yl", "x"),
    )
    group, plane = ("zh", "zl"), ("yh", "yl", "x")
    tokens = group + plane
    return jax.shard_map(
        per_device,
        mesh=grid,
        in_specs=(
            P(tokens, None),
            P(tokens, None),
            P(tokens, None),
            P(tokens, None),
            P(plane, None, "pool"),
            P(plane, None, "pool"),
            P(plane, "pool", None),
            P(plane, group),
        ),
        out_specs=(P(tokens, "pool"), P(plane, ("pool",) + group)),
        check_vma=False,
    )
```

```python
import jax
import jax.numpy as jnp
from jax import lax
from jax.experimental import pallas as pl
from jax.experimental.pallas import tpu as pltpu
from jax.sharding import Mesh, PartitionSpec as P

ROWS = 8
SORT = 256
Z_BLOCKS = 4
BF = jnp.bfloat16
F32 = jnp.float32


def dot_f32(left, right):
    return jnp.dot(left, right, preferred_element_type=F32)


def dot_transposed(left, right):
    return lax.dot_general(left, right, (((1,), (1,)), ((), ())), preferred_element_type=F32)


def moved(rows_out, rows_in, source):
    at = lax.broadcasted_iota(jnp.int32, (rows_out, rows_in), 0)
    of = lax.broadcasted_iota(jnp.int32, (rows_out, rows_in), 1)
    return (of == source(at)).astype(BF)


def expert_kernel(rows_ref, *refs):
    weights, out_ref, held, sems = refs[:6], refs[6], refs[7:13], refs[13]
    copies = [pltpu.make_async_copy(w, h, sems.at[i]) for i, (w, h) in enumerate(zip(weights, held))]
    for copy in copies:
        copy.start()
    total_rows, piece = rows_ref.shape
    width = held[0].shape[0]
    parts = 2 * width // piece
    block = min(SORT, total_rows)
    slots = block // parts
    to_parts = moved(block, block, lambda i: lax.rem(i, slots) * parts + lax.div(i, slots))
    sorted_rows = [
        dot_f32(to_parts, rows_ref[i:i + block]).astype(BF) for i in range(0, total_rows, block)
    ]
    part = [
        jnp.concatenate([rows[i * slots:(i + 1) * slots] for rows in sorted_rows], axis=0)
        for i in range(parts)
    ]
    inputs_rows = jnp.concatenate(part[:parts // 2], axis=1)
    grads_rows = jnp.concatenate(part[parts // 2:], axis=1)
    total = None
    for half in range(2):
        gate_ref, up_ref, down_ref = held[3 * half:3 * half + 3]
        copies[3 * half].wait()
        gate_value = dot_f32(inputs_rows, gate_ref[...])
        copies[3 * half + 1].wait()
        up_value = dot_f32(inputs_rows, up_ref[...])
        copies[3 * half + 2].wait()
        act_grad = dot_transposed(grads_rows, down_ref[...])
        sigmoid_gate = jax.nn.sigmoid(gate_value)
        up_grad = (act_grad * gate_value * sigmoid_gate).astype(BF)
        gate_grad = (
            act_grad * up_value * sigmoid_gate * (1.0 + gate_value * (1.0 - sigmoid_gate))
        ).astype(BF)
        half_grad = dot_transposed(gate_grad, gate_ref[...]) + dot_transposed(up_grad, up_ref[...])
        total = half_grad if total is None else total + half_grad
    total = total.astype(BF)
    back = out_ref.shape[1]
    pieces = width // back
    block = min(SORT, out_ref.shape[0])
    slots = block // pieces
    to_slots = moved(block, block, lambda i: lax.rem(i, pieces) * slots + lax.div(i, pieces))
    for at in range(out_ref.shape[0] // block):
        rows = total[at * slots:(at + 1) * slots]
        stacked = jnp.concatenate([rows[:, i * back:(i + 1) * back] for i in range(pieces)], axis=0)
        out_ref[at * block:(at + 1) * block] = dot_f32(to_slots, stacked).astype(BF)


def expert_rows(rows, weights, back):
    width = weights[0].shape[0]
    slots = rows.size // (2 * width)
    hidden = weights[0].shape[1]
    vmem = pl.BlockSpec(memory_space=pltpu.VMEM)
    anywhere = pl.BlockSpec(memory_space=pltpu.HBM)
    return pl.pallas_call(
        expert_kernel,
        out_shape=jax.ShapeDtypeStruct((slots * width // back, back), BF),
        in_specs=[vmem] + [anywhere] * 6,
        out_specs=vmem,
        scratch_shapes=[pltpu.VMEM(w.shape, BF) for w in weights] + [pltpu.SemaphoreType.DMA((6,))],
        compiler_params=pltpu.CompilerParams(vmem_limit_bytes=50 * 2**20),
        cost_estimate=pl.CostEstimate(
            flops=2 * slots * width * hidden * 10,
            bytes_accessed=12 * width * hidden,
            transcendentals=2 * slots * hidden,
        ),
        name="expert",
    )(rows, *weights)


def product_kernel(place_ref, *refs):
    contexts, tokens_ref, out_ref = refs[:-2], refs[-2], refs[-1]
    peers, depth, width = tokens_ref.shape
    tok = depth // len(contexts)
    total = None
    for i, ref in enumerate(contexts):
        tokens = tokens_ref[:, i * tok:(i + 1) * tok, :].reshape(peers * tok, width)
        term = dot_f32(ref[...], tokens)
        total = term if total is None else total + term
    blocks, heads, cols = out_ref.shape
    z_blocks = width // cols
    y_blocks = blocks // z_blocks
    yh_index = place_ref[0]
    for z in range(z_blocks):
        for apart in range(y_blocks):
            out_ref[jnp.bitwise_xor(yh_index, apart) * z_blocks + z] = total[
                apart * heads:(apart + 1) * heads, z * cols:(z + 1) * cols
            ].astype(BF)


def context_product(yh_index, contexts, tokens_b, y_blocks, z_blocks):
    rows, depth = contexts[0].shape
    width = tokens_b.shape[2]
    return pl.pallas_call(
        product_kernel,
        out_shape=jax.ShapeDtypeStruct((y_blocks * z_blocks, rows // y_blocks, width // z_blocks), BF),
        in_specs=[pl.BlockSpec(memory_space=pltpu.SMEM)]
        + [pl.BlockSpec(memory_space=pltpu.VMEM)] * (len(contexts) + 1),
        out_specs=pl.BlockSpec(memory_space=pltpu.VMEM),
        compiler_params=pltpu.CompilerParams(vmem_limit_bytes=16 * 2**20),
        cost_estimate=pl.CostEstimate(
            flops=2 * len(contexts) * rows * depth * width,
            bytes_accessed=2 * len(contexts) * depth * (rows + width),
            transcendentals=0,
        ),
        name="context_product",
    )(yh_index.astype(jnp.int32).reshape(1), *contexts, tokens_b)


def finish_kernel(zl_ref, mine_ref, came_ref, grad_ref, hidden_ref, keep_ref, send_ref):
    parts, _, width = mine_ref.shape
    for i in range(parts):
        at = slice(i * width, (i + 1) * width)
        hidden_ref[:, at] = grad_ref[:, at].astype(F32) + (mine_ref[i] + came_ref[i])
    first = zl_ref[0] == 0
    cols = hidden_ref.shape[1] // (2 * Z_BLOCKS)
    for z in range(Z_BLOCKS):
        even = hidden_ref[:, 2 * z * cols:(2 * z + 1) * cols]
        odd = hidden_ref[:, (2 * z + 1) * cols:(2 * z + 2) * cols]
        at = slice(z * cols, (z + 1) * cols)
        keep_ref[:, at] = jnp.where(first, even, odd).astype(BF)
        send_ref[:, at] = jnp.where(first, odd, even).astype(BF)


def finish(zl_index, mine, came, grad_half):
    tok, width = grad_half.shape
    vmem = pl.BlockSpec(memory_space=pltpu.VMEM)
    half = jax.ShapeDtypeStruct((tok, width // 2), BF)
    return pl.pallas_call(
        finish_kernel,
        out_shape=(jax.ShapeDtypeStruct((tok, width), F32), half, half),
        in_specs=[pl.BlockSpec(memory_space=pltpu.SMEM)] + [vmem] * 3,
        out_specs=(vmem,) * 3,
        compiler_params=pltpu.CompilerParams(vmem_limit_bytes=8 * 2**20),
        cost_estimate=pl.CostEstimate(flops=3 * tok * width, bytes_accessed=16 * tok * width, transcendentals=0),
        name="finish",
    )(zl_index.astype(jnp.int32).reshape(1), mine, came, grad_half)


def swap_pool(value):
    return lax.ppermute(value, "pool", ((0, 1), (1, 0)))


def exchange(value, axes):
    return lax.all_to_all(value, axes, split_axis=0, concat_axis=0, tiled=True)


def swapped(value, axis, size, bit):
    return lax.ppermute(value, axis, tuple((s, s ^ bit) for s in range(size)))


def context_blocks(context_t, yh_index, y_blocks):
    wide = context_t.shape[1] // y_blocks
    return [
        lax.dynamic_slice_in_dim(context_t, jnp.bitwise_xor(yh_index, r) * wide, wide, 1)
        for r in range(y_blocks)
    ]


def swap_places(pieces, bit):
    y_blocks, heads = len(pieces[0]), pieces[0][0].shape[0]
    crossing = [(i, r) for i in range(len(pieces)) for r in range(y_blocks) if r & bit]
    came = swapped(jnp.concatenate([pieces[i][r] for i, r in crossing], axis=0), "yh", y_blocks, bit)
    pieces = [list(places) for places in pieces]
    for at, (i, r) in enumerate(crossing):
        pieces[i][r] = came[at * heads:(at + 1) * heads]
    return pieces


def per_device(moe_in, out_grad, gates, routes, w_gate, w_up, w_down, context_t):
    tok_rows, model_width = moe_in.shape
    top_count = routes.shape[1]
    plane = ("yh", "yl", "x")
    experts = lax.axis_size(plane)
    y_blocks, z_blocks = lax.axis_size("yh"), lax.axis_size("zh")
    peers = experts // y_blocks
    capacity = 2 * tok_rows * top_count // experts
    own_slots = capacity // 2
    pool_index = lax.axis_index("pool")
    yh_index, zl_index = lax.axis_index("yh"), lax.axis_index("zl")
    half_width = model_width // 2
    pair_count = tok_rows * top_count

    expert_ids = routes.reshape(pair_count)
    hits = (expert_ids[:, None] == jnp.arange(experts, dtype=jnp.int32)[None, :]).astype(jnp.int32)
    earlier = jnp.cumsum(hits, axis=0) - hits
    position = jnp.sum(earlier * hits, axis=1)
    own = position // own_slots == pool_index
    slot_ids = jnp.where(own, expert_ids * own_slots + position % own_slots, -1)
    slot_ids = slot_ids.reshape(tok_rows, top_count)
    slot_grid = jnp.arange(experts * own_slots, dtype=jnp.int32)
    placed = slot_ids[:, :, None] == slot_grid[None, None, :]
    picker = jnp.any(placed, axis=1).astype(BF)
    weights = jnp.sum(jnp.where(placed, gates[:, :, None], 0.0), axis=1)

    piece_width = 2 * model_width * own_slots // ROWS
    parts = 2 * model_width // piece_width
    stacked = jnp.concatenate(
        [a[:, i * piece_width:(i + 1) * piece_width] for a in (moe_in, out_grad) for i in range(parts // 2)], 0
    )
    eye = jnp.eye(parts, dtype=BF)
    spread = (picker.T[:, None, None, :] * eye[None, :, :, None]).reshape(
        experts * ROWS, parts * tok_rows
    )
    send = dot_f32(spread, stacked).astype(BF).reshape(experts, ROWS, piece_width)
    heads = context_t.shape[0]
    [places] = swap_places([context_blocks(context_t, yh_index, y_blocks)], 2)
    send, weights, places = lax.optimization_barrier((send, weights, places))
    received = exchange(send, plane)
    other_gate, other_up, other_down = swap_pool(w_gate[0]), swap_pool(w_up[0]), swap_pool(w_down[0])
    beside = swapped(jnp.concatenate(places, axis=0), "zl", 2, 1)
    received, beside = lax.optimization_barrier((received, beside))
    pieces = [places, [beside[r * heads:(r + 1) * heads] for r in range(y_blocks)]]

    back_width = model_width * own_slots // ROWS
    back_parts = model_width // back_width
    back = expert_rows(
        received.reshape(experts * ROWS, piece_width),
        (w_gate[0], w_up[0], w_down[0], other_gate, other_up, other_down),
        back_width,
    ).reshape(experts, ROWS, back_width)
    returned = exchange(back, plane)
    contexts = [jnp.concatenate(piece, axis=0) for piece in swap_places(pieces, 1)]
    returned, contexts = lax.optimization_barrier((returned, contexts))

    high = lax.reduce_precision(weights, 8, 7).astype(BF)
    low = (weights - high.astype(F32)).astype(BF)
    both = jnp.stack((high, low))
    back_eye = jnp.eye(back_parts, dtype=BF)
    mixer = (both[None, :, :, :, None] * back_eye[:, None, None, None, :]).reshape(
        back_parts * 2 * tok_rows, experts * ROWS
    )
    mixed = dot_f32(mixer, returned.reshape(experts * ROWS, back_width))
    mixed = jnp.sum(mixed.reshape(back_parts, 2, tok_rows, back_width), axis=1)
    per_half = back_parts // 2
    mine = lax.dynamic_slice_in_dim(mixed, pool_index * per_half, per_half, 0)
    theirs = lax.dynamic_slice_in_dim(mixed, (1 - pool_index) * per_half, per_half, 0)
    grad_half = lax.dynamic_slice_in_dim(out_grad, pool_index * half_width, half_width, 1)
    hidden_grad, keep, give = finish(zl_index, mine, swap_pool(theirs), grad_half)
    pair = jnp.concatenate((keep, swapped(give, "zl", 2, 1)), axis=0)
    gathered_b = exchange(jnp.broadcast_to(pair[None], (peers, *pair.shape)), ("yl", "x"))
    terms = exchange(
        context_product(yh_index, contexts, gathered_b, y_blocks, z_blocks), ("yh", "zh")
    )
    wo_grad = jnp.sum(terms.astype(F32), axis=0)
    return (hidden_grad, wo_grad)


def solution(mesh):
    pool, group, ep = (mesh.shape[name] for name in ("pool", "group", "ep"))
    y_blocks, x_size = 4, 8
    grid = Mesh(
        mesh.devices.reshape(pool, Z_BLOCKS, group // Z_BLOCKS, y_blocks, ep // (y_blocks * x_size), x_size),
        ("pool", "zh", "zl", "yh", "yl", "x"),
    )
    group, plane = ("zh", "zl"), ("yh", "yl", "x")
    tokens = group + plane
    return jax.shard_map(
        per_device,
        mesh=grid,
        in_specs=(
            P(tokens, None),
            P(tokens, None),
            P(tokens, None),
            P(tokens, None),
            P(plane, None, "pool"),
            P(plane, None, "pool"),
            P(plane, "pool", None),
            P(plane, group),
        ),
        out_specs=(P(tokens, "pool"), P(plane, ("pool",) + group)),
        check_vma=False,
    )
```

```python
import jax
import jax.numpy as jnp
from jax import lax
from jax.experimental import pallas as pl
from jax.experimental.pallas import tpu as pltpu
from jax.sharding import Mesh, PartitionSpec as P

ROWS = 8
SORT = 256
Z_BLOCKS = 4
BF = jnp.bfloat16
F32 = jnp.float32


def dot_f32(left, right):
    return jnp.dot(left, right, preferred_element_type=F32)


def dot_transposed(left, right):
    return lax.dot_general(left, right, (((1,), (1,)), ((), ())), preferred_element_type=F32)


def moved(rows_out, rows_in, source):
    at = lax.broadcasted_iota(jnp.int32, (rows_out, rows_in), 0)
    of = lax.broadcasted_iota(jnp.int32, (rows_out, rows_in), 1)
    return (of == source(at)).astype(BF)


def expert_kernel(rows_ref, *refs):
    weights, out_ref, held, sems = refs[:6], refs[6], refs[7:13], refs[13]
    copies = [pltpu.make_async_copy(w, h, sems.at[i]) for i, (w, h) in enumerate(zip(weights, held))]
    for copy in copies:
        copy.start()
    total_rows, piece = rows_ref.shape
    width = held[0].shape[0]
    parts = 2 * width // piece
    block = min(SORT, total_rows)
    slots = block // parts
    to_parts = moved(block, block, lambda i: lax.rem(i, slots) * parts + lax.div(i, slots))
    sorted_rows = [
        dot_f32(to_parts, rows_ref[i:i + block]).astype(BF) for i in range(0, total_rows, block)
    ]
    part = [
        jnp.concatenate([rows[i * slots:(i + 1) * slots] for rows in sorted_rows], axis=0)
        for i in range(parts)
    ]
    inputs_rows = jnp.concatenate(part[:parts // 2], axis=1)
    grads_rows = jnp.concatenate(part[parts // 2:], axis=1)
    total = None
    for half in range(2):
        gate_ref, up_ref, down_ref = held[3 * half:3 * half + 3]
        copies[3 * half].wait()
        gate_value = dot_f32(inputs_rows, gate_ref[...])
        copies[3 * half + 1].wait()
        up_value = dot_f32(inputs_rows, up_ref[...])
        copies[3 * half + 2].wait()
        act_grad = dot_transposed(grads_rows, down_ref[...])
        sigmoid_gate = jax.nn.sigmoid(gate_value)
        up_grad = (act_grad * gate_value * sigmoid_gate).astype(BF)
        gate_grad = (
            act_grad * up_value * sigmoid_gate * (1.0 + gate_value * (1.0 - sigmoid_gate))
        ).astype(BF)
        half_grad = dot_transposed(gate_grad, gate_ref[...]) + dot_transposed(up_grad, up_ref[...])
        total = half_grad if total is None else total + half_grad
    total = total.astype(BF)
    back = out_ref.shape[1]
    pieces = width // back
    block = min(SORT, out_ref.shape[0])
    slots = block // pieces
    to_slots = moved(block, block, lambda i: lax.rem(i, pieces) * slots + lax.div(i, pieces))
    for at in range(out_ref.shape[0] // block):
        rows = total[at * slots:(at + 1) * slots]
        stacked = jnp.concatenate([rows[:, i * back:(i + 1) * back] for i in range(pieces)], axis=0)
        out_ref[at * block:(at + 1) * block] = dot_f32(to_slots, stacked).astype(BF)


def expert_rows(rows, weights, back):
    width = weights[0].shape[0]
    slots = rows.size // (2 * width)
    hidden = weights[0].shape[1]
    vmem = pl.BlockSpec(memory_space=pltpu.VMEM)
    anywhere = pl.BlockSpec(memory_space=pltpu.HBM)
    return pl.pallas_call(
        expert_kernel,
        out_shape=jax.ShapeDtypeStruct((slots * width // back, back), BF),
        in_specs=[vmem] + [anywhere] * 6,
        out_specs=vmem,
        scratch_shapes=[pltpu.VMEM(w.shape, BF) for w in weights] + [pltpu.SemaphoreType.DMA((6,))],
        compiler_params=pltpu.CompilerParams(vmem_limit_bytes=50 * 2**20),
        cost_estimate=pl.CostEstimate(
            flops=2 * slots * width * hidden * 10,
            bytes_accessed=12 * width * hidden,
            transcendentals=2 * slots * hidden,
        ),
        name="expert",
    )(rows, *weights)


def product_kernel(place_ref, *refs):
    contexts, tokens_ref, out_ref = refs[:-2], refs[-2], refs[-1]
    peers, tok, width = tokens_ref.shape
    peers //= len(contexts)
    yh_index, zl_index = place_ref[0], place_ref[1]
    total = None
    for apart, ref in enumerate(contexts):
        tokens = tokens_ref[pl.ds(jnp.bitwise_xor(zl_index, apart) * peers, peers)]
        term = dot_f32(ref[...], tokens.reshape(peers * tok, width))
        total = term if total is None else total + term
    blocks, heads, cols = out_ref.shape
    z_blocks = width // cols
    y_blocks = blocks // z_blocks
    for z in range(z_blocks):
        for apart in range(y_blocks):
            out_ref[jnp.bitwise_xor(yh_index, apart) * z_blocks + z] = total[
                apart * heads:(apart + 1) * heads, z * cols:(z + 1) * cols
            ].astype(BF)


def context_product(place, contexts, tokens_b, y_blocks, z_blocks):
    rows, depth = contexts[0].shape
    width = tokens_b.shape[2]
    return pl.pallas_call(
        product_kernel,
        out_shape=jax.ShapeDtypeStruct((y_blocks * z_blocks, rows // y_blocks, width // z_blocks), BF),
        in_specs=[pl.BlockSpec(memory_space=pltpu.SMEM)]
        + [pl.BlockSpec(memory_space=pltpu.VMEM)] * (len(contexts) + 1),
        out_specs=pl.BlockSpec(memory_space=pltpu.VMEM),
        compiler_params=pltpu.CompilerParams(vmem_limit_bytes=16 * 2**20),
        cost_estimate=pl.CostEstimate(
            flops=2 * len(contexts) * rows * depth * width,
            bytes_accessed=2 * len(contexts) * depth * (rows + width),
            transcendentals=0,
        ),
        name="context_product",
    )(place, *contexts, tokens_b)


def finish_kernel(mine_ref, came_ref, grad_ref, hidden_ref, spread_ref):
    parts, _, width = mine_ref.shape
    for i in range(parts):
        at = slice(i * width, (i + 1) * width)
        hidden_ref[:, at] = grad_ref[:, at].astype(F32) + (mine_ref[i] + came_ref[i])
    blocks, _, held = spread_ref.shape
    cols = held // Z_BLOCKS
    pair = hidden_ref.shape[1] // held
    for z in range(Z_BLOCKS):
        for of in range(pair):
            at = (pair * z + of) * cols
            rounded = hidden_ref[:, at:at + cols].astype(BF)
            for peer in range(blocks // pair):
                spread_ref[of * (blocks // pair) + peer, :, z * cols:(z + 1) * cols] = rounded


def finish(mine, came, grad_half, peers):
    tok, width = grad_half.shape
    vmem = pl.BlockSpec(memory_space=pltpu.VMEM)
    return pl.pallas_call(
        finish_kernel,
        out_shape=(
            jax.ShapeDtypeStruct((tok, width), F32),
            jax.ShapeDtypeStruct((2 * peers, tok, width // 2), BF),
        ),
        in_specs=[vmem] * 3,
        out_specs=(vmem,) * 2,
        compiler_params=pltpu.CompilerParams(vmem_limit_bytes=8 * 2**20),
        cost_estimate=pl.CostEstimate(
            flops=3 * tok * width, bytes_accessed=(16 + 2 * peers) * tok * width, transcendentals=0
        ),
        name="finish",
    )(mine, came, grad_half)


def swap_pool(value):
    return lax.ppermute(value, "pool", ((0, 1), (1, 0)))


def exchange(value, axes):
    return lax.all_to_all(value, axes, split_axis=0, concat_axis=0, tiled=True)


def swapped(value, axis, size, bit):
    return lax.ppermute(value, axis, tuple((s, s ^ bit) for s in range(size)))


def context_blocks(context_t, yh_index, y_blocks):
    wide = context_t.shape[1] // y_blocks
    return [
        lax.dynamic_slice_in_dim(context_t, jnp.bitwise_xor(yh_index, r) * wide, wide, 1)
        for r in range(y_blocks)
    ]


def swap_places(pieces, bit):
    y_blocks, heads = len(pieces[0]), pieces[0][0].shape[0]
    crossing = [(i, r) for i in range(len(pieces)) for r in range(y_blocks) if r & bit]
    came = swapped(jnp.concatenate([pieces[i][r] for i, r in crossing], axis=0), "yh", y_blocks, bit)
    pieces = [list(places) for places in pieces]
    for at, (i, r) in enumerate(crossing):
        pieces[i][r] = came[at * heads:(at + 1) * heads]
    return pieces


def per_device(moe_in, out_grad, gates, routes, w_gate, w_up, w_down, context_t):
    tok_rows, model_width = moe_in.shape
    top_count = routes.shape[1]
    plane = ("yh", "yl", "x")
    experts = lax.axis_size(plane)
    y_blocks, z_blocks = lax.axis_size("yh"), lax.axis_size("zh")
    peers = experts // y_blocks
    capacity = 2 * tok_rows * top_count // experts
    own_slots = capacity // 2
    pool_index = lax.axis_index("pool")
    yh_index, zl_index = lax.axis_index("yh"), lax.axis_index("zl")
    half_width = model_width // 2
    pair_count = tok_rows * top_count

    expert_ids = routes.reshape(pair_count)
    hits = (expert_ids[:, None] == jnp.arange(experts, dtype=jnp.int32)[None, :]).astype(jnp.int32)
    earlier = jnp.cumsum(hits, axis=0) - hits
    position = jnp.sum(earlier * hits, axis=1)
    own = position // own_slots == pool_index
    slot_ids = jnp.where(own, expert_ids * own_slots + position % own_slots, -1)
    slot_ids = slot_ids.reshape(tok_rows, top_count)
    slot_grid = jnp.arange(experts * own_slots, dtype=jnp.int32)
    placed = slot_ids[:, :, None] == slot_grid[None, None, :]
    picker = jnp.any(placed, axis=1).astype(BF)
    weights = jnp.sum(jnp.where(placed, gates[:, :, None], 0.0), axis=1)

    piece_width = 2 * model_width * own_slots // ROWS
    parts = 2 * model_width // piece_width
    stacked = jnp.concatenate(
        [a[:, i * piece_width:(i + 1) * piece_width] for a in (moe_in, out_grad) for i in range(parts // 2)], 0
    )
    eye = jnp.eye(parts, dtype=BF)
    spread = (picker.T[:, None, None, :] * eye[None, :, :, None]).reshape(
        experts * ROWS, parts * tok_rows
    )
    send = dot_f32(spread, stacked).astype(BF).reshape(experts, ROWS, piece_width)
    heads = context_t.shape[0]
    [places] = swap_places([context_blocks(context_t, yh_index, y_blocks)], 1)
    send, weights, places = lax.optimization_barrier((send, weights, places))
    received = exchange(send, plane)
    other_gate, other_up, other_down = swap_pool(w_gate[0]), swap_pool(w_up[0]), swap_pool(w_down[0])
    beside = swapped(jnp.concatenate(places, axis=0), "zl", 2, 1)
    received, beside = lax.optimization_barrier((received, beside))
    pieces = [places, [beside[r * heads:(r + 1) * heads] for r in range(y_blocks)]]

    back_width = model_width * own_slots // ROWS
    back_parts = model_width // back_width
    back = expert_rows(
        received.reshape(experts * ROWS, piece_width),
        (w_gate[0], w_up[0], w_down[0], other_gate, other_up, other_down),
        back_width,
    ).reshape(experts, ROWS, back_width)
    returned = exchange(back, plane)
    contexts = [jnp.concatenate(piece, axis=0) for piece in swap_places(pieces, 2)]
    returned, contexts = lax.optimization_barrier((returned, contexts))

    high = lax.reduce_precision(weights, 8, 7).astype(BF)
    low = (weights - high.astype(F32)).astype(BF)
    both = jnp.stack((high, low))
    back_eye = jnp.eye(back_parts, dtype=BF)
    mixer = (both[None, :, :, :, None] * back_eye[:, None, None, None, :]).reshape(
        back_parts * 2 * tok_rows, experts * ROWS
    )
    mixed = dot_f32(mixer, returned.reshape(experts * ROWS, back_width))
    mixed = jnp.sum(mixed.reshape(back_parts, 2, tok_rows, back_width), axis=1)
    per_half = back_parts // 2
    mine = lax.dynamic_slice_in_dim(mixed, pool_index * per_half, per_half, 0)
    theirs = lax.dynamic_slice_in_dim(mixed, (1 - pool_index) * per_half, per_half, 0)
    grad_half = lax.dynamic_slice_in_dim(out_grad, pool_index * half_width, half_width, 1)
    hidden_grad, columns = finish(mine, swap_pool(theirs), grad_half, peers)
    gathered_b = exchange(columns, ("zl", "yl", "x"))
    place = jnp.stack([yh_index, zl_index]).astype(jnp.int32)
    terms = exchange(
        context_product(place, contexts, gathered_b, y_blocks, z_blocks), ("yh", "zh")
    )
    wo_grad = jnp.sum(terms.astype(F32), axis=0)
    return (hidden_grad, wo_grad)


def solution(mesh):
    pool, group, ep = (mesh.shape[name] for name in ("pool", "group", "ep"))
    y_blocks, x_size = 4, 8
    grid = Mesh(
        mesh.devices.reshape(pool, Z_BLOCKS, group // Z_BLOCKS, y_blocks, ep // (y_blocks * x_size), x_size),
        ("pool", "zh", "zl", "yh", "yl", "x"),
    )
    group, plane = ("zh", "zl"), ("yh", "yl", "x")
    tokens = group + plane
    return jax.shard_map(
        per_device,
        mesh=grid,
        in_specs=(
            P(tokens, None),
            P(tokens, None),
            P(tokens, None),
            P(tokens, None),
            P(plane, None, "pool"),
            P(plane, None, "pool"),
            P(plane, "pool", None),
            P(plane, group),
        ),
        out_specs=(P(tokens, "pool"), P(plane, ("pool",) + group)),
        check_vma=False,
    )
```

```python
import jax
import jax.numpy as jnp
from jax import lax
from jax.experimental import pallas as pl
from jax.experimental.pallas import tpu as pltpu
from jax.sharding import Mesh, PartitionSpec as P

ROWS = 8
SORT = 256
Z_BLOCKS = 4
BF = jnp.bfloat16
F32 = jnp.float32


def dot_f32(left, right):
    return jnp.dot(left, right, preferred_element_type=F32)


def dot_transposed(left, right):
    return lax.dot_general(left, right, (((1,), (1,)), ((), ())), preferred_element_type=F32)


def moved(rows_out, rows_in, source):
    at = lax.broadcasted_iota(jnp.int32, (rows_out, rows_in), 0)
    of = lax.broadcasted_iota(jnp.int32, (rows_out, rows_in), 1)
    return (of == source(at)).astype(BF)


def expert_kernel(rows_ref, *refs):
    weights, out_ref, held, sems = refs[:6], refs[6], refs[7:13], refs[13]
    copies = [pltpu.make_async_copy(w, h, sems.at[i]) for i, (w, h) in enumerate(zip(weights, held))]
    for copy in copies:
        copy.start()
    total_rows, piece = rows_ref.shape
    width = held[0].shape[0]
    parts = 2 * width // piece
    block = min(SORT, total_rows)
    slots = block // parts
    to_parts = moved(block, block, lambda i: lax.rem(i, slots) * parts + lax.div(i, slots))
    sorted_rows = [
        dot_f32(to_parts, rows_ref[i:i + block]).astype(BF) for i in range(0, total_rows, block)
    ]
    part = [
        jnp.concatenate([rows[i * slots:(i + 1) * slots] for rows in sorted_rows], axis=0)
        for i in range(parts)
    ]
    inputs_rows = jnp.concatenate(part[:parts // 2], axis=1)
    grads_rows = jnp.concatenate(part[parts // 2:], axis=1)
    total = None
    for half in range(2):
        gate_ref, up_ref, down_ref = held[3 * half:3 * half + 3]
        copies[3 * half].wait()
        gate_value = dot_f32(inputs_rows, gate_ref[...])
        copies[3 * half + 1].wait()
        up_value = dot_f32(inputs_rows, up_ref[...])
        copies[3 * half + 2].wait()
        act_grad = dot_transposed(grads_rows, down_ref[...])
        sigmoid_gate = jax.nn.sigmoid(gate_value)
        up_grad = (act_grad * gate_value * sigmoid_gate).astype(BF)
        gate_grad = (
            act_grad * up_value * sigmoid_gate * (1.0 + gate_value * (1.0 - sigmoid_gate))
        ).astype(BF)
        half_grad = dot_transposed(gate_grad, gate_ref[...]) + dot_transposed(up_grad, up_ref[...])
        total = half_grad if total is None else total + half_grad
    total = total.astype(BF)
    back = out_ref.shape[1]
    pieces = width // back
    block = min(SORT, out_ref.shape[0])
    slots = block // pieces
    to_slots = moved(block, block, lambda i: lax.rem(i, pieces) * slots + lax.div(i, pieces))
    for at in range(out_ref.shape[0] // block):
        rows = total[at * slots:(at + 1) * slots]
        stacked = jnp.concatenate([rows[:, i * back:(i + 1) * back] for i in range(pieces)], axis=0)
        out_ref[at * block:(at + 1) * block] = dot_f32(to_slots, stacked).astype(BF)


def expert_rows(rows, weights, back):
    width = weights[0].shape[0]
    slots = rows.size // (2 * width)
    hidden = weights[0].shape[1]
    vmem = pl.BlockSpec(memory_space=pltpu.VMEM)
    anywhere = pl.BlockSpec(memory_space=pltpu.HBM)
    return pl.pallas_call(
        expert_kernel,
        out_shape=jax.ShapeDtypeStruct((slots * width // back, back), BF),
        in_specs=[vmem] + [anywhere] * 6,
        out_specs=vmem,
        scratch_shapes=[pltpu.VMEM(w.shape, BF) for w in weights] + [pltpu.SemaphoreType.DMA((6,))],
        compiler_params=pltpu.CompilerParams(vmem_limit_bytes=50 * 2**20),
        cost_estimate=pl.CostEstimate(
            flops=2 * slots * width * hidden * 10,
            bytes_accessed=12 * width * hidden,
            transcendentals=2 * slots * hidden,
        ),
        name="expert",
    )(rows, *weights)


def product_kernel(place_ref, *refs):
    contexts, tokens_ref, out_ref = refs[:-2], refs[-2], refs[-1]
    peers, tok, width = tokens_ref.shape
    peers //= len(contexts)
    yh_index, zl_index = place_ref[0], place_ref[1]
    total = None
    for apart, ref in enumerate(contexts):
        tokens = tokens_ref[pl.ds(jnp.bitwise_xor(zl_index, apart) * peers, peers)]
        term = dot_f32(ref[...], tokens.reshape(peers * tok, width))
        total = term if total is None else total + term
    blocks, heads, cols = out_ref.shape
    z_blocks = width // cols
    y_blocks = blocks // z_blocks
    for z in range(z_blocks):
        for apart in range(y_blocks):
            out_ref[jnp.bitwise_xor(yh_index, apart) * z_blocks + z] = total[
                apart * heads:(apart + 1) * heads, z * cols:(z + 1) * cols
            ].astype(BF)


def context_product(place, contexts, tokens_b, y_blocks, z_blocks):
    rows, depth = contexts[0].shape
    width = tokens_b.shape[2]
    return pl.pallas_call(
        product_kernel,
        out_shape=jax.ShapeDtypeStruct((y_blocks * z_blocks, rows // y_blocks, width // z_blocks), BF),
        in_specs=[pl.BlockSpec(memory_space=pltpu.SMEM)]
        + [pl.BlockSpec(memory_space=pltpu.VMEM)] * (len(contexts) + 1),
        out_specs=pl.BlockSpec(memory_space=pltpu.VMEM),
        compiler_params=pltpu.CompilerParams(vmem_limit_bytes=16 * 2**20),
        cost_estimate=pl.CostEstimate(
            flops=2 * len(contexts) * rows * depth * width,
            bytes_accessed=2 * len(contexts) * depth * (rows + width),
            transcendentals=0,
        ),
        name="context_product",
    )(place, *contexts, tokens_b)


def finish_kernel(mine_ref, came_ref, grad_ref, hidden_ref, spread_ref):
    parts, _, width = mine_ref.shape
    for i in range(parts):
        at = slice(i * width, (i + 1) * width)
        hidden_ref[:, at] = grad_ref[:, at].astype(F32) + (mine_ref[i] + came_ref[i])
    blocks, _, held = spread_ref.shape
    cols = held // Z_BLOCKS
    pair = hidden_ref.shape[1] // held
    for z in range(Z_BLOCKS):
        for of in range(pair):
            at = (pair * z + of) * cols
            rounded = hidden_ref[:, at:at + cols].astype(BF)
            for peer in range(blocks // pair):
                spread_ref[of * (blocks // pair) + peer, :, z * cols:(z + 1) * cols] = rounded


def finish(mine, came, grad_half, peers):
    tok, width = grad_half.shape
    vmem = pl.BlockSpec(memory_space=pltpu.VMEM)
    return pl.pallas_call(
        finish_kernel,
        out_shape=(
            jax.ShapeDtypeStruct((tok, width), F32),
            jax.ShapeDtypeStruct((2 * peers, tok, width // 2), BF),
        ),
        in_specs=[vmem] * 3,
        out_specs=(vmem,) * 2,
        compiler_params=pltpu.CompilerParams(vmem_limit_bytes=8 * 2**20),
        cost_estimate=pl.CostEstimate(
            flops=3 * tok * width, bytes_accessed=(16 + 2 * peers) * tok * width, transcendentals=0
        ),
        name="finish",
    )(mine, came, grad_half)


def swap_pool(value):
    return lax.ppermute(value, "pool", ((0, 1), (1, 0)))


def exchange(value, axes):
    return lax.all_to_all(value, axes, split_axis=0, concat_axis=0, tiled=True)


def swapped(value, axis, size, bit):
    return lax.ppermute(value, axis, tuple((s, s ^ bit) for s in range(size)))


def context_blocks(context_t, yh_index, y_blocks):
    wide = context_t.shape[1] // y_blocks
    return [
        lax.dynamic_slice_in_dim(context_t, jnp.bitwise_xor(yh_index, r) * wide, wide, 1)
        for r in range(y_blocks)
    ]


def swap_places(pieces, bit):
    y_blocks, heads = len(pieces[0]), pieces[0][0].shape[0]
    crossing = [(i, r) for i in range(len(pieces)) for r in range(y_blocks) if r & bit]
    came = swapped(jnp.concatenate([pieces[i][r] for i, r in crossing], axis=0), "yh", y_blocks, bit)
    pieces = [list(places) for places in pieces]
    for at, (i, r) in enumerate(crossing):
        pieces[i][r] = came[at * heads:(at + 1) * heads]
    return pieces


def per_device(moe_in, out_grad, gates, routes, w_gate, w_up, w_down, context_t):
    tok_rows, model_width = moe_in.shape
    top_count = routes.shape[1]
    plane = ("yh", "yl", "x")
    experts = lax.axis_size(plane)
    y_blocks, z_blocks = lax.axis_size("yh"), lax.axis_size("zh")
    peers = experts // y_blocks
    capacity = 2 * tok_rows * top_count // experts
    own_slots = capacity // 2
    pool_index = lax.axis_index("pool")
    yh_index, zl_index = lax.axis_index("yh"), lax.axis_index("zl")
    half_width = model_width // 2
    pair_count = tok_rows * top_count

    expert_ids = routes.reshape(pair_count)
    hits = (expert_ids[:, None] == jnp.arange(experts, dtype=jnp.int32)[None, :]).astype(jnp.int32)
    earlier = jnp.cumsum(hits, axis=0) - hits
    position = jnp.sum(earlier * hits, axis=1)
    own = position // own_slots == pool_index
    slot_ids = jnp.where(own, expert_ids * own_slots + position % own_slots, -1)
    slot_ids = slot_ids.reshape(tok_rows, top_count)
    slot_grid = jnp.arange(experts * own_slots, dtype=jnp.int32)
    placed = slot_ids[:, :, None] == slot_grid[None, None, :]
    picker = jnp.any(placed, axis=1).astype(BF)
    weights = jnp.sum(jnp.where(placed, gates[:, :, None], 0.0), axis=1)

    piece_width = 2 * model_width * own_slots // ROWS
    parts = 2 * model_width // piece_width
    stacked = jnp.concatenate(
        [a[:, i * piece_width:(i + 1) * piece_width] for a in (moe_in, out_grad) for i in range(parts // 2)], 0
    )
    eye = jnp.eye(parts, dtype=BF)
    spread = (picker.T[:, None, None, :] * eye[None, :, :, None]).reshape(
        experts * ROWS, parts * tok_rows
    )
    send = dot_f32(spread, stacked).astype(BF).reshape(experts, ROWS, piece_width)
    send, weights, context_t = lax.optimization_barrier((send, weights, context_t))
    received = exchange(send, plane)
    other_gate, other_up, other_down = swap_pool(w_gate[0]), swap_pool(w_up[0]), swap_pool(w_down[0])
    beside = swapped(context_t, "zl", 2, 1)
    received, beside = lax.optimization_barrier((received, beside))

    back_width = model_width * own_slots // ROWS
    back_parts = model_width // back_width
    back = expert_rows(
        received.reshape(experts * ROWS, piece_width),
        (w_gate[0], w_up[0], w_down[0], other_gate, other_up, other_down),
        back_width,
    ).reshape(experts, ROWS, back_width)
    returned = exchange(back, plane)
    pieces = [context_blocks(piece, yh_index, y_blocks) for piece in (context_t, beside)]
    pieces = swap_places(pieces, 1)
    returned, pieces = lax.optimization_barrier((returned, pieces))

    high = lax.reduce_precision(weights, 8, 7).astype(BF)
    low = (weights - high.astype(F32)).astype(BF)
    both = jnp.stack((high, low))
    back_eye = jnp.eye(back_parts, dtype=BF)
    mixer = (both[None, :, :, :, None] * back_eye[:, None, None, None, :]).reshape(
        back_parts * 2 * tok_rows, experts * ROWS
    )
    mixed = dot_f32(mixer, returned.reshape(experts * ROWS, back_width))
    mixed = jnp.sum(mixed.reshape(back_parts, 2, tok_rows, back_width), axis=1)
    per_half = back_parts // 2
    mine = lax.dynamic_slice_in_dim(mixed, pool_index * per_half, per_half, 0)
    theirs = lax.dynamic_slice_in_dim(mixed, (1 - pool_index) * per_half, per_half, 0)
    grad_half = lax.dynamic_slice_in_dim(out_grad, pool_index * half_width, half_width, 1)
    hidden_grad, columns = finish(mine, swap_pool(theirs), grad_half, peers)
    gathered_b = exchange(columns, ("zl", "yl", "x"))
    contexts = [jnp.concatenate(piece, axis=0) for piece in swap_places(pieces, 2)]
    place = jnp.stack([yh_index, zl_index]).astype(jnp.int32)
    terms = exchange(
        context_product(place, contexts, gathered_b, y_blocks, z_blocks), ("yh", "zh")
    )
    wo_grad = jnp.sum(terms.astype(F32), axis=0)
    return (hidden_grad, wo_grad)


def solution(mesh):
    pool, group, ep = (mesh.shape[name] for name in ("pool", "group", "ep"))
    y_blocks, x_size = 4, 8
    grid = Mesh(
        mesh.devices.reshape(pool, Z_BLOCKS, group // Z_BLOCKS, y_blocks, ep // (y_blocks * x_size), x_size),
        ("pool", "zh", "zl", "yh", "yl", "x"),
    )
    group, plane = ("zh", "zl"), ("yh", "yl", "x")
    tokens = group + plane
    return jax.shard_map(
        per_device,
        mesh=grid,
        in_specs=(
            P(tokens, None),
            P(tokens, None),
            P(tokens, None),
            P(tokens, None),
            P(plane, None, "pool"),
            P(plane, None, "pool"),
            P(plane, "pool", None),
            P(plane, group),
        ),
        out_specs=(P(tokens, "pool"), P(plane, ("pool",) + group)),
        check_vma=False,
    )
```

```python
import jax
import jax.numpy as jnp
from jax import lax
from jax.experimental import pallas as pl
from jax.experimental.pallas import tpu as pltpu
from jax.sharding import Mesh, PartitionSpec as P

ROWS = 8
SORT = 256
Z_BLOCKS = 8
BF = jnp.bfloat16
F32 = jnp.float32


def dot_f32(left, right):
    return jnp.dot(left, right, preferred_element_type=F32)


def dot_transposed(left, right):
    return lax.dot_general(left, right, (((1,), (1,)), ((), ())), preferred_element_type=F32)


def moved(rows_out, rows_in, source):
    at = lax.broadcasted_iota(jnp.int32, (rows_out, rows_in), 0)
    of = lax.broadcasted_iota(jnp.int32, (rows_out, rows_in), 1)
    return (of == source(at)).astype(BF)


def expert_kernel(rows_ref, *refs):
    weights, out_ref, held, sems = refs[:6], refs[6], refs[7:13], refs[13]
    copies = [pltpu.make_async_copy(w, h, sems.at[i]) for i, (w, h) in enumerate(zip(weights, held))]
    for copy in copies:
        copy.start()
    total_rows, piece = rows_ref.shape
    width = held[0].shape[0]
    parts = 2 * width // piece
    block = min(SORT, total_rows)
    slots = block // parts
    to_parts = moved(block, block, lambda i: lax.rem(i, slots) * parts + lax.div(i, slots))
    sorted_rows = [
        dot_f32(to_parts, rows_ref[i:i + block]).astype(BF) for i in range(0, total_rows, block)
    ]
    part = [
        jnp.concatenate([rows[i * slots:(i + 1) * slots] for rows in sorted_rows], axis=0)
        for i in range(parts)
    ]
    inputs_rows = jnp.concatenate(part[:parts // 2], axis=1)
    grads_rows = jnp.concatenate(part[parts // 2:], axis=1)
    total = None
    for half in range(2):
        gate_ref, up_ref, down_ref = held[3 * half:3 * half + 3]
        copies[3 * half].wait()
        gate_value = dot_f32(inputs_rows, gate_ref[...])
        copies[3 * half + 1].wait()
        up_value = dot_f32(inputs_rows, up_ref[...])
        copies[3 * half + 2].wait()
        act_grad = dot_transposed(grads_rows, down_ref[...])
        sigmoid_gate = jax.nn.sigmoid(gate_value)
        up_grad = (act_grad * gate_value * sigmoid_gate).astype(BF)
        gate_grad = (
            act_grad * up_value * sigmoid_gate * (1.0 + gate_value * (1.0 - sigmoid_gate))
        ).astype(BF)
        half_grad = dot_transposed(gate_grad, gate_ref[...]) + dot_transposed(up_grad, up_ref[...])
        total = half_grad if total is None else total + half_grad
    total = total.astype(BF)
    back = out_ref.shape[1]
    pieces = width // back
    block = min(SORT, out_ref.shape[0])
    slots = block // pieces
    to_slots = moved(block, block, lambda i: lax.rem(i, pieces) * slots + lax.div(i, pieces))
    for at in range(out_ref.shape[0] // block):
        rows = total[at * slots:(at + 1) * slots]
        stacked = jnp.concatenate([rows[:, i * back:(i + 1) * back] for i in range(pieces)], axis=0)
        out_ref[at * block:(at + 1) * block] = dot_f32(to_slots, stacked).astype(BF)


def expert_rows(rows, weights, back):
    width = weights[0].shape[0]
    slots = rows.size // (2 * width)
    hidden = weights[0].shape[1]
    vmem = pl.BlockSpec(memory_space=pltpu.VMEM)
    anywhere = pl.BlockSpec(memory_space=pltpu.HBM)
    return pl.pallas_call(
        expert_kernel,
        out_shape=jax.ShapeDtypeStruct((slots * width // back, back), BF),
        in_specs=[vmem] + [anywhere] * 6,
        out_specs=vmem,
        scratch_shapes=[pltpu.VMEM(w.shape, BF) for w in weights] + [pltpu.SemaphoreType.DMA((6,))],
        compiler_params=pltpu.CompilerParams(vmem_limit_bytes=50 * 2**20),
        cost_estimate=pl.CostEstimate(
            flops=2 * slots * width * hidden * 10,
            bytes_accessed=12 * width * hidden,
            transcendentals=2 * slots * hidden,
        ),
        name="expert",
    )(rows, *weights)


def product_kernel(place_ref, *refs):
    contexts, tokens_ref, out_ref = refs[:-2], refs[-2], refs[-1]
    peers, tok, width = tokens_ref.shape
    peers //= len(contexts)
    yh_index, zl_index = place_ref[0], place_ref[1]
    total = None
    for apart, ref in enumerate(contexts):
        tokens = tokens_ref[pl.ds(jnp.bitwise_xor(zl_index, apart) * peers, peers)]
        term = dot_f32(ref[...], tokens.reshape(peers * tok, width))
        total = term if total is None else total + term
    blocks, heads, cols = out_ref.shape
    z_blocks = width // cols
    y_blocks = blocks // z_blocks
    for z in range(z_blocks):
        for apart in range(y_blocks):
            out_ref[jnp.bitwise_xor(yh_index, apart) * z_blocks + z] = total[
                apart * heads:(apart + 1) * heads, z * cols:(z + 1) * cols
            ].astype(BF)


def context_product(place, contexts, tokens_b, y_blocks, z_blocks):
    rows, depth = contexts[0].shape
    width = tokens_b.shape[2]
    return pl.pallas_call(
        product_kernel,
        out_shape=jax.ShapeDtypeStruct((y_blocks * z_blocks, rows // y_blocks, width // z_blocks), BF),
        in_specs=[pl.BlockSpec(memory_space=pltpu.SMEM)]
        + [pl.BlockSpec(memory_space=pltpu.VMEM)] * (len(contexts) + 1),
        out_specs=pl.BlockSpec(memory_space=pltpu.VMEM),
        compiler_params=pltpu.CompilerParams(vmem_limit_bytes=16 * 2**20),
        cost_estimate=pl.CostEstimate(
            flops=2 * len(contexts) * rows * depth * width,
            bytes_accessed=2 * len(contexts) * depth * (rows + width),
            transcendentals=0,
        ),
        name="context_product",
    )(place, *contexts, tokens_b)


def finish_kernel(mine_ref, came_ref, grad_ref, hidden_ref, spread_ref):
    parts, _, width = mine_ref.shape
    for i in range(parts):
        at = slice(i * width, (i + 1) * width)
        hidden_ref[:, at] = grad_ref[:, at].astype(F32) + (mine_ref[i] + came_ref[i])
    blocks, _, held = spread_ref.shape
    cols = held // Z_BLOCKS
    pair = hidden_ref.shape[1] // held
    for z in range(Z_BLOCKS):
        for of in range(pair):
            at = (pair * z + of) * cols
            rounded = hidden_ref[:, at:at + cols].astype(BF)
            for peer in range(blocks // pair):
                spread_ref[of * (blocks // pair) + peer, :, z * cols:(z + 1) * cols] = rounded


def finish(mine, came, grad_half, peers):
    tok, width = grad_half.shape
    vmem = pl.BlockSpec(memory_space=pltpu.VMEM)
    return pl.pallas_call(
        finish_kernel,
        out_shape=(
            jax.ShapeDtypeStruct((tok, width), F32),
            jax.ShapeDtypeStruct((peers, tok, width), BF),
        ),
        in_specs=[vmem] * 3,
        out_specs=(vmem,) * 2,
        compiler_params=pltpu.CompilerParams(vmem_limit_bytes=8 * 2**20),
        cost_estimate=pl.CostEstimate(
            flops=3 * tok * width, bytes_accessed=(16 + 2 * peers) * tok * width, transcendentals=0
        ),
        name="finish",
    )(mine, came, grad_half)


def swap_pool(value):
    return lax.ppermute(value, "pool", ((0, 1), (1, 0)))


def exchange(value, axes):
    return lax.all_to_all(value, axes, split_axis=0, concat_axis=0, tiled=True)


def swapped(value, axis, size, bit):
    return lax.ppermute(value, axis, tuple((s, s ^ bit) for s in range(size)))


def context_blocks(context_t, yh_index, y_blocks):
    wide = context_t.shape[1] // y_blocks
    return [
        lax.dynamic_slice_in_dim(context_t, jnp.bitwise_xor(yh_index, r) * wide, wide, 1)
        for r in range(y_blocks)
    ]


def swap_places(pieces, bit):
    y_blocks, heads = len(pieces[0]), pieces[0][0].shape[0]
    crossing = [(i, r) for i in range(len(pieces)) for r in range(y_blocks) if r & bit]
    came = swapped(jnp.concatenate([pieces[i][r] for i, r in crossing], axis=0), "yh", y_blocks, bit)
    pieces = [list(places) for places in pieces]
    for at, (i, r) in enumerate(crossing):
        pieces[i][r] = came[at * heads:(at + 1) * heads]
    return pieces


def per_device(moe_in, out_grad, gates, routes, w_gate, w_up, w_down, context_t):
    tok_rows, model_width = moe_in.shape
    top_count = routes.shape[1]
    plane = ("yh", "yl", "x")
    experts = lax.axis_size(plane)
    y_blocks, z_blocks = lax.axis_size("yh"), lax.axis_size("zh")
    peers = experts // y_blocks
    capacity = 2 * tok_rows * top_count // experts
    own_slots = capacity // 2
    pool_index = lax.axis_index("pool")
    yh_index, zl_index = lax.axis_index("yh"), lax.axis_index("zl")
    half_width = model_width // 2
    pair_count = tok_rows * top_count

    expert_ids = routes.reshape(pair_count)
    hits = (expert_ids[:, None] == jnp.arange(experts, dtype=jnp.int32)[None, :]).astype(jnp.int32)
    earlier = jnp.cumsum(hits, axis=0) - hits
    position = jnp.sum(earlier * hits, axis=1)
    own = position // own_slots == pool_index
    slot_ids = jnp.where(own, expert_ids * own_slots + position % own_slots, -1)
    slot_ids = slot_ids.reshape(tok_rows, top_count)
    slot_grid = jnp.arange(experts * own_slots, dtype=jnp.int32)
    placed = slot_ids[:, :, None] == slot_grid[None, None, :]
    picker = jnp.any(placed, axis=1).astype(BF)
    weights = jnp.sum(jnp.where(placed, gates[:, :, None], 0.0), axis=1)

    piece_width = 2 * model_width * own_slots // ROWS
    parts = 2 * model_width // piece_width
    stacked = jnp.concatenate(
        [a[:, i * piece_width:(i + 1) * piece_width] for a in (moe_in, out_grad) for i in range(parts // 2)], 0
    )
    eye = jnp.eye(parts, dtype=BF)
    spread = (picker.T[:, None, None, :] * eye[None, :, :, None]).reshape(
        experts * ROWS, parts * tok_rows
    )
    send = dot_f32(spread, stacked).astype(BF).reshape(experts, ROWS, piece_width)
    send, weights, context_t = lax.optimization_barrier((send, weights, context_t))
    received = exchange(send, plane)
    other_gate, other_up, other_down = swap_pool(w_gate[0]), swap_pool(w_up[0]), swap_pool(w_down[0])

    back_width = model_width * own_slots // ROWS
    back_parts = model_width // back_width
    back = expert_rows(
        received.reshape(experts * ROWS, piece_width),
        (w_gate[0], w_up[0], w_down[0], other_gate, other_up, other_down),
        back_width,
    ).reshape(experts, ROWS, back_width)
    back, context_t = lax.optimization_barrier((back, context_t))
    returned = exchange(back, plane)
    pieces = [context_blocks(context_t, yh_index, y_blocks)]
    pieces = swap_places(pieces, 1)
    returned, pieces = lax.optimization_barrier((returned, pieces))

    high = lax.reduce_precision(weights, 8, 7).astype(BF)
    low = (weights - high.astype(F32)).astype(BF)
    both = jnp.stack((high, low))
    back_eye = jnp.eye(back_parts, dtype=BF)
    mixer = (both[None, :, :, :, None] * back_eye[:, None, None, None, :]).reshape(
        back_parts * 2 * tok_rows, experts * ROWS
    )
    mixed = dot_f32(mixer, returned.reshape(experts * ROWS, back_width))
    mixed = jnp.sum(mixed.reshape(back_parts, 2, tok_rows, back_width), axis=1)
    per_half = back_parts // 2
    mine = lax.dynamic_slice_in_dim(mixed, pool_index * per_half, per_half, 0)
    theirs = lax.dynamic_slice_in_dim(mixed, (1 - pool_index) * per_half, per_half, 0)
    grad_half = lax.dynamic_slice_in_dim(out_grad, pool_index * half_width, half_width, 1)
    hidden_grad, columns = finish(mine, swap_pool(theirs), grad_half, peers)
    gathered_b = exchange(columns, ("zl", "yl", "x"))
    contexts = [jnp.concatenate(piece, axis=0) for piece in swap_places(pieces, 2)]
    place = jnp.stack([yh_index, zl_index]).astype(jnp.int32)
    terms = exchange(
        context_product(place, contexts, gathered_b, y_blocks, z_blocks), ("yh", "zh")
    )
    wo_grad = jnp.sum(terms.astype(F32), axis=0)
    return (hidden_grad, wo_grad)


def solution(mesh):
    pool, group, ep = (mesh.shape[name] for name in ("pool", "group", "ep"))
    y_blocks, x_size = 4, 8
    grid = Mesh(
        mesh.devices.reshape(pool, Z_BLOCKS, group // Z_BLOCKS, y_blocks, ep // (y_blocks * x_size), x_size),
        ("pool", "zh", "zl", "yh", "yl", "x"),
    )
    group, plane = ("zh", "zl"), ("yh", "yl", "x")
    tokens = group + plane
    return jax.shard_map(
        per_device,
        mesh=grid,
        in_specs=(
            P(tokens, None),
            P(tokens, None),
            P(tokens, None),
            P(tokens, None),
            P(plane, None, "pool"),
            P(plane, None, "pool"),
            P(plane, "pool", None),
            P(plane, group),
        ),
        out_specs=(P(tokens, "pool"), P(plane, ("pool",) + group)),
        check_vma=False,
    )
```

```python
import jax
import jax.numpy as jnp
from jax import lax
from jax.experimental import pallas as pl
from jax.experimental.pallas import tpu as pltpu
from jax.sharding import Mesh, PartitionSpec as P

ROWS = 8
SORT = 256
Z_BLOCKS = 8
BF = jnp.bfloat16
F32 = jnp.float32


def dot_f32(left, right):
    return jnp.dot(left, right, preferred_element_type=F32)


def dot_transposed(left, right):
    return lax.dot_general(left, right, (((1,), (1,)), ((), ())), preferred_element_type=F32)


def moved(rows_out, rows_in, source):
    at = lax.broadcasted_iota(jnp.int32, (rows_out, rows_in), 0)
    of = lax.broadcasted_iota(jnp.int32, (rows_out, rows_in), 1)
    return (of == source(at)).astype(BF)


def expert_kernel(rows_ref, *refs):
    weights, out_ref, held, sems = refs[:6], refs[6], refs[7:13], refs[13]
    copies = [pltpu.make_async_copy(w, h, sems.at[i]) for i, (w, h) in enumerate(zip(weights, held))]
    for copy in copies:
        copy.start()
    total_rows, piece = rows_ref.shape
    width = held[0].shape[0]
    parts = 2 * width // piece
    block = min(SORT, total_rows)
    slots = block // parts
    to_parts = moved(block, block, lambda i: lax.rem(i, slots) * parts + lax.div(i, slots))
    sorted_rows = [
        dot_f32(to_parts, rows_ref[i:i + block]).astype(BF) for i in range(0, total_rows, block)
    ]
    part = [
        jnp.concatenate([rows[i * slots:(i + 1) * slots] for rows in sorted_rows], axis=0)
        for i in range(parts)
    ]
    inputs_rows = jnp.concatenate(part[:parts // 2], axis=1)
    grads_rows = jnp.concatenate(part[parts // 2:], axis=1)
    total = None
    for half in range(2):
        gate_ref, up_ref, down_ref = held[3 * half:3 * half + 3]
        copies[3 * half].wait()
        gate_value = dot_f32(inputs_rows, gate_ref[...])
        copies[3 * half + 1].wait()
        up_value = dot_f32(inputs_rows, up_ref[...])
        copies[3 * half + 2].wait()
        act_grad = dot_transposed(grads_rows, down_ref[...])
        sigmoid_gate = jax.nn.sigmoid(gate_value)
        up_grad = (act_grad * gate_value * sigmoid_gate).astype(BF)
        gate_grad = (
            act_grad * up_value * sigmoid_gate * (1.0 + gate_value * (1.0 - sigmoid_gate))
        ).astype(BF)
        half_grad = dot_transposed(gate_grad, gate_ref[...]) + dot_transposed(up_grad, up_ref[...])
        total = half_grad if total is None else total + half_grad
    total = total.astype(BF)
    back = out_ref.shape[1]
    pieces = width // back
    block = min(SORT, out_ref.shape[0])
    slots = block // pieces
    to_slots = moved(block, block, lambda i: lax.rem(i, pieces) * slots + lax.div(i, pieces))
    for at in range(out_ref.shape[0] // block):
        rows = total[at * slots:(at + 1) * slots]
        stacked = jnp.concatenate([rows[:, i * back:(i + 1) * back] for i in range(pieces)], axis=0)
        out_ref[at * block:(at + 1) * block] = dot_f32(to_slots, stacked).astype(BF)


def expert_rows(rows, weights, back):
    width = weights[0].shape[0]
    slots = rows.size // (2 * width)
    hidden = weights[0].shape[1]
    vmem = pl.BlockSpec(memory_space=pltpu.VMEM)
    anywhere = pl.BlockSpec(memory_space=pltpu.HBM)
    return pl.pallas_call(
        expert_kernel,
        out_shape=jax.ShapeDtypeStruct((slots * width // back, back), BF),
        in_specs=[vmem] + [anywhere] * 6,
        out_specs=vmem,
        scratch_shapes=[pltpu.VMEM(w.shape, BF) for w in weights] + [pltpu.SemaphoreType.DMA((6,))],
        compiler_params=pltpu.CompilerParams(vmem_limit_bytes=50 * 2**20),
        cost_estimate=pl.CostEstimate(
            flops=2 * slots * width * hidden * 10,
            bytes_accessed=12 * width * hidden,
            transcendentals=2 * slots * hidden,
        ),
        name="expert",
    )(rows, *weights)


def product_kernel(place_ref, *refs):
    contexts, tokens_ref, out_ref = refs[:-2], refs[-2], refs[-1]
    peers, tok, width = tokens_ref.shape
    peers //= len(contexts)
    yh_index, zl_index = place_ref[0], place_ref[1]
    total = None
    for apart, ref in enumerate(contexts):
        tokens = tokens_ref[pl.ds(jnp.bitwise_xor(zl_index, apart) * peers, peers)]
        term = dot_f32(ref[...], tokens.reshape(peers * tok, width))
        total = term if total is None else total + term
    blocks, heads, cols = out_ref.shape
    z_blocks = width // cols
    y_blocks = blocks // z_blocks
    for z in range(z_blocks):
        for apart in range(y_blocks):
            out_ref[z * y_blocks + jnp.bitwise_xor(yh_index, apart)] = total[
                apart * heads:(apart + 1) * heads, z * cols:(z + 1) * cols
            ].astype(BF)


def context_product(place, contexts, tokens_b, y_blocks, z_blocks):
    rows, depth = contexts[0].shape
    width = tokens_b.shape[2]
    return pl.pallas_call(
        product_kernel,
        out_shape=jax.ShapeDtypeStruct((z_blocks * y_blocks, rows // y_blocks, width // z_blocks), BF),
        in_specs=[pl.BlockSpec(memory_space=pltpu.SMEM)]
        + [pl.BlockSpec(memory_space=pltpu.VMEM)] * (len(contexts) + 1),
        out_specs=pl.BlockSpec(memory_space=pltpu.VMEM),
        compiler_params=pltpu.CompilerParams(vmem_limit_bytes=16 * 2**20),
        cost_estimate=pl.CostEstimate(
            flops=2 * len(contexts) * rows * depth * width,
            bytes_accessed=2 * len(contexts) * depth * (rows + width),
            transcendentals=0,
        ),
        name="context_product",
    )(place, *contexts, tokens_b)


def finish_kernel(mine_ref, came_ref, grad_ref, hidden_ref, spread_ref):
    parts, _, width = mine_ref.shape
    for i in range(parts):
        at = slice(i * width, (i + 1) * width)
        hidden_ref[:, at] = grad_ref[:, at].astype(F32) + (mine_ref[i] + came_ref[i])
    blocks, _, held = spread_ref.shape
    cols = held // Z_BLOCKS
    pair = hidden_ref.shape[1] // held
    for z in range(Z_BLOCKS):
        for of in range(pair):
            at = (pair * z + of) * cols
            rounded = hidden_ref[:, at:at + cols].astype(BF)
            for peer in range(blocks // pair):
                spread_ref[of * (blocks // pair) + peer, :, z * cols:(z + 1) * cols] = rounded


def finish(mine, came, grad_half, peers):
    tok, width = grad_half.shape
    vmem = pl.BlockSpec(memory_space=pltpu.VMEM)
    return pl.pallas_call(
        finish_kernel,
        out_shape=(
            jax.ShapeDtypeStruct((tok, width), F32),
            jax.ShapeDtypeStruct((peers, tok, width), BF),
        ),
        in_specs=[vmem] * 3,
        out_specs=(vmem,) * 2,
        compiler_params=pltpu.CompilerParams(vmem_limit_bytes=8 * 2**20),
        cost_estimate=pl.CostEstimate(
            flops=3 * tok * width, bytes_accessed=(16 + 2 * peers) * tok * width, transcendentals=0
        ),
        name="finish",
    )(mine, came, grad_half)


def swap_pool(value):
    return lax.ppermute(value, "pool", ((0, 1), (1, 0)))


def exchange(value, axes):
    return lax.all_to_all(value, axes, split_axis=0, concat_axis=0, tiled=True)


def swapped(value, axis, size, bit):
    return lax.ppermute(value, axis, tuple((s, s ^ bit) for s in range(size)))


def context_blocks(context_t, yh_index, y_blocks):
    wide = context_t.shape[1] // y_blocks
    return [
        lax.dynamic_slice_in_dim(context_t, jnp.bitwise_xor(yh_index, r) * wide, wide, 1)
        for r in range(y_blocks)
    ]


def swap_places(pieces, bit):
    y_blocks, heads = len(pieces[0]), pieces[0][0].shape[0]
    crossing = [(i, r) for i in range(len(pieces)) for r in range(y_blocks) if r & bit]
    came = swapped(jnp.concatenate([pieces[i][r] for i, r in crossing], axis=0), "yh", y_blocks, bit)
    pieces = [list(places) for places in pieces]
    for at, (i, r) in enumerate(crossing):
        pieces[i][r] = came[at * heads:(at + 1) * heads]
    return pieces


def per_device(moe_in, out_grad, gates, routes, w_gate, w_up, w_down, context_t):
    tok_rows, model_width = moe_in.shape
    top_count = routes.shape[1]
    plane = ("yh", "yl", "x")
    experts = lax.axis_size(plane)
    y_blocks, z_blocks = lax.axis_size("yh"), lax.axis_size("zh")
    peers = experts // y_blocks
    capacity = 2 * tok_rows * top_count // experts
    own_slots = capacity // 2
    pool_index = lax.axis_index("pool")
    yh_index, zl_index = lax.axis_index("yh"), lax.axis_index("zl")
    half_width = model_width // 2
    pair_count = tok_rows * top_count

    expert_ids = routes.reshape(pair_count)
    hits = (expert_ids[:, None] == jnp.arange(experts, dtype=jnp.int32)[None, :]).astype(jnp.int32)
    earlier = jnp.cumsum(hits, axis=0) - hits
    position = jnp.sum(earlier * hits, axis=1)
    own = position // own_slots == pool_index
    slot_ids = jnp.where(own, expert_ids * own_slots + position % own_slots, -1)
    slot_ids = slot_ids.reshape(tok_rows, top_count)
    slot_grid = jnp.arange(experts * own_slots, dtype=jnp.int32)
    placed = slot_ids[:, :, None] == slot_grid[None, None, :]
    picker = jnp.any(placed, axis=1).astype(BF)
    weights = jnp.sum(jnp.where(placed, gates[:, :, None], 0.0), axis=1)

    piece_width = 2 * model_width * own_slots // ROWS
    parts = 2 * model_width // piece_width
    stacked = jnp.concatenate(
        [a[:, i * piece_width:(i + 1) * piece_width] for a in (moe_in, out_grad) for i in range(parts // 2)], 0
    )
    eye = jnp.eye(parts, dtype=BF)
    spread = (picker.T[:, None, None, :] * eye[None, :, :, None]).reshape(
        experts * ROWS, parts * tok_rows
    )
    send = dot_f32(spread, stacked).astype(BF).reshape(experts, ROWS, piece_width)
    send, weights, context_t = lax.optimization_barrier((send, weights, context_t))
    received = exchange(send, plane)
    other_gate, other_up, other_down = swap_pool(w_gate[0]), swap_pool(w_up[0]), swap_pool(w_down[0])

    back_width = model_width * own_slots // ROWS
    back_parts = model_width // back_width
    back = expert_rows(
        received.reshape(experts * ROWS, piece_width),
        (w_gate[0], w_up[0], w_down[0], other_gate, other_up, other_down),
        back_width,
    ).reshape(experts, ROWS, back_width)
    back, context_t = lax.optimization_barrier((back, context_t))
    returned = exchange(back, plane)
    pieces = [context_blocks(context_t, yh_index, y_blocks)]
    pieces = swap_places(pieces, 1)
    returned, pieces = lax.optimization_barrier((returned, pieces))

    high = lax.reduce_precision(weights, 8, 7).astype(BF)
    low = (weights - high.astype(F32)).astype(BF)
    both = jnp.stack((high, low))
    back_eye = jnp.eye(back_parts, dtype=BF)
    mixer = (both[None, :, :, :, None] * back_eye[:, None, None, None, :]).reshape(
        back_parts * 2 * tok_rows, experts * ROWS
    )
    mixed = dot_f32(mixer, returned.reshape(experts * ROWS, back_width))
    mixed = jnp.sum(mixed.reshape(back_parts, 2, tok_rows, back_width), axis=1)
    per_half = back_parts // 2
    mine = lax.dynamic_slice_in_dim(mixed, pool_index * per_half, per_half, 0)
    theirs = lax.dynamic_slice_in_dim(mixed, (1 - pool_index) * per_half, per_half, 0)
    grad_half = lax.dynamic_slice_in_dim(out_grad, pool_index * half_width, half_width, 1)
    hidden_grad, columns = finish(mine, swap_pool(theirs), grad_half, peers)
    gathered_b = exchange(columns, ("zl", "yl", "x"))
    contexts = [jnp.concatenate(piece, axis=0) for piece in swap_places(pieces, 2)]
    place = jnp.stack([yh_index, zl_index]).astype(jnp.int32)
    terms = exchange(
        context_product(place, contexts, gathered_b, y_blocks, z_blocks), ("zh", "yh")
    )
    wo_grad = jnp.sum(terms.astype(F32), axis=0)
    return (hidden_grad, wo_grad)


def solution(mesh):
    pool, group, ep = (mesh.shape[name] for name in ("pool", "group", "ep"))
    y_blocks, x_size = 4, 8
    grid = Mesh(
        mesh.devices.reshape(pool, Z_BLOCKS, group // Z_BLOCKS, y_blocks, ep // (y_blocks * x_size), x_size),
        ("pool", "zh", "zl", "yh", "yl", "x"),
    )
    group, plane = ("zh", "zl"), ("yh", "yl", "x")
    tokens = group + plane
    return jax.shard_map(
        per_device,
        mesh=grid,
        in_specs=(
            P(tokens, None),
            P(tokens, None),
            P(tokens, None),
            P(tokens, None),
            P(plane, None, "pool"),
            P(plane, None, "pool"),
            P(plane, "pool", None),
            P(plane, group),
        ),
        out_specs=(P(tokens, "pool"), P(plane, ("pool",) + group)),
        check_vma=False,
    )
```
